32 devices in a mesh: seq: 8 (over z, x), tp: 4 (over y, core).
Axes of the slice: x: 2, y: 2, z: 4, core: 2. Of those that a mesh axis runs over, the one named last changes fastest.
Arguments:
- token_ids: int32 [8192], P('seq'), may hold values from 0 to 511
- embed_table: bfloat16 [512, 2048], P(None, 'tp'), may hold values from -6 to 6
- norm_gain: float32 [2048], replicated, may hold values from 0.1 to 1.9
- in_weight: bfloat16 [2048, 3, 2048], P('seq', None, 'tp'), may hold values from -0.125 to 0.125
- short_filter: float32 [7, 3, 2048], P(None, None, 'tp'), may hold values from -2.4 to 2.4
- long_filter: bfloat16 [128, 128], P('tp'), may hold values from -0.5390625 to 0.5390625
- long_skip: float32 [2048], P('tp'), may hold values from -3 to 3
- out_weight: bfloat16 [2048, 2048], P('tp', 'seq'), may hold values from -0.125 to 0.125
Outputs:
- mixed: bfloat16 [8192, 2048], P('seq', 'tp')
The draws below stay inside these ranges and needn't reach their ends.
All inputs are finite; a program needn't handle non-finite values.
Results may differ from the reference program's by a relative error of at most 0.012.
Values may be sent and summed in bfloat16 or wider, within the bound.
No kernel may reach another device: no remote copies, remote signals or barrier semaphores. Data moves between devices by JAX's collectives and lax.ppermute only.
A program may use at most 64 MiB of HBM per device.

```python
import math
import jax
import jax.numpy as jnp
import numpy as np
from jax import lax

D = 2048
VOCAB = 512
GROUP = 16
TAPS = 128
SHORT = 7
TOKENS = 8192
GROUPS = 128
N_TP = 4


def plant(entries, rng, smallest, top_value):
    longest = entries.shape.index(max(entries.shape))
    spots = []
    for shift in (0, 1):
        where = [jax.random.randint(jax.random.fold_in(rng, axis), (), 0, length) for axis, length in enumerate(entries.shape)]
        where[longest] = (where[longest] + shift) % entries.shape[longest]
        spots.append(tuple(where))
    return entries.at[spots[0]].set(smallest).at[spots[1]].set(top_value)


def levels(own_key, extent, shards, least, high):
    loudness = 1.0
    for dim, shards_of in shards:
        heights = jax.random.uniform(jax.random.fold_in(jax.random.fold_in(own_key, 6), dim), (shards_of,), jnp.float32, least / len(shards), high / len(shards))
        loudness = loudness * jnp.repeat(jnp.exp(heights), extent[dim] // shards_of).reshape((-1,) + (1,) * (len(extent) - 1 - dim))
    return loudness


def cumulative_ranks(count, slope):
    portions = [(1 << 20) // math.isqrt(grade ** slope) + 1 for grade in range(1, count + 1)]
    width = 1 + sum(portions) // (1 << 30)
    return np.cumsum(np.array([max(1, weight // width) for weight in portions]))


def ranked_ids(own_key, extent, amount, skew):
    listing = cumulative_ranks(amount, skew)
    ticket = jax.random.randint(jax.random.fold_in(own_key, 1), extent, 0, int(listing[amount - 1]))
    grade = jnp.searchsorted(jnp.asarray(listing, jnp.int32), ticket, side="right")
    return jax.random.permutation(jax.random.fold_in(own_key, 2), amount)[grade].astype(jnp.int32)


def scatter_about(rng, dims, spread, bound, cuts=(), kind=jnp.bfloat16):
    result = spread * jax.random.normal(rng, dims, jnp.float32)
    if cuts:
        result = result * levels(rng, dims, cuts, -0.22, 0.18)
    return jnp.clip(result, -bound, bound).astype(kind)


def setup_inputs(seed: int = 0) -> dict:
    arg_keys = jax.random.split(jax.random.key(seed), 9)
    token_ids = plant(ranked_ids(arg_keys[0], (TOKENS,), VOCAB, 2), jax.random.fold_in(arg_keys[0], 3), 0, VOCAB - 1).astype(jnp.int32)
    embed_table = scatter_about(arg_keys[1], (VOCAB, D), 1.0, 6.0, ((1, 4),))
    norm_gain = jnp.clip(1.0 + 0.18 * jax.random.normal(arg_keys[2], (D,), jnp.float32), 0.1, 1.9)
    in_weight = scatter_about(arg_keys[3], (D, 3, D), D ** -0.5, 0.125, ((0, 8), (2, 4)))
    short_filter = scatter_about(arg_keys[4], (SHORT, 3, D), 0.4, 2.4, ((2, 4),), jnp.float32)
    long_filter = scatter_about(arg_keys[5], (GROUPS, TAPS), 0.09, 0.5390625, ((0, 4),))
    long_skip = scatter_about(arg_keys[6], (D,), 0.7, 3.0, ((0, 4),), jnp.float32)
    out_weight = scatter_about(arg_keys[7], (D, D), D ** -0.5, 0.125, ((0, 4), (1, 8)))
    return {"token_ids": token_ids, "embed_table": embed_table, "norm_gain": norm_gain, "in_weight": in_weight, "short_filter": short_filter, "long_filter": long_filter, "long_skip": long_skip, "out_weight": out_weight}


def reference(token_ids, embed_table, norm_gain, in_weight, short_filter, long_filter, long_skip, out_weight):
    embedded = embed_table[token_ids]
    widened = embedded.astype(jnp.float32)
    scaled = widened * lax.rsqrt(lax.optimization_barrier(jnp.mean(widened * widened, axis=1, keepdims=True)) + 1e-06) * norm_gain[None, :]
    normed = scaled.astype(jnp.bfloat16)
    tok_total = normed.shape[0]
    projected = jnp.dot(normed, in_weight.reshape(D, 3 * D), preferred_element_type=jnp.float32)
    projected = projected.astype(jnp.bfloat16).reshape(tok_total, 3, D)
    padded = jnp.pad(projected, ((SHORT - 1, 0), (0, 0), (0, 0)))
    featured = jnp.zeros((tok_total, 3, D), jnp.float32)
    for tap_index in range(SHORT):
        begin = SHORT - 1 - tap_index
        featured = featured + short_filter[tap_index][None] * padded[begin:begin + tok_total].astype(jnp.float32)
    queries = featured[:, 0]
    product = (featured[:, 1] * featured[:, 2]).astype(jnp.bfloat16)
    taps_wide = jnp.repeat(long_filter.astype(jnp.float32), GROUP, axis=0)
    source = jnp.pad(product.astype(jnp.float32), ((TAPS - 1, 0), (0, 0)))

    def add_lag(tap_index, running):
        column = lax.dynamic_slice_in_dim(taps_wide, tap_index.astype(jnp.int32), 1, 1)[:, 0]
        begin = (TAPS - 1 - tap_index).astype(jnp.int32)
        return running + column[None, :] * lax.dynamic_slice_in_dim(source, begin, tok_total, 0)
    convolved = lax.fori_loop(0, TAPS, add_lag, jnp.zeros((tok_total, D), jnp.float32))
    convolved = convolved + long_skip[None, :] * product.astype(jnp.float32)
    gated = (queries * convolved).astype(jnp.bfloat16)
    band_width = D // N_TP
    running = jnp.zeros((tok_total, D), jnp.float32)
    for block_index in range(N_TP):
        lower = block_index * band_width
        partial_term = jnp.dot(gated[:, lower:lower + band_width], out_weight[lower:lower + band_width], preferred_element_type=jnp.float32).astype(jnp.bfloat16)
        partial_term = lax.optimization_barrier(partial_term)
        running = running + partial_term.astype(jnp.float32)
    return (widened + running).astype(jnp.bfloat16)
```

```python
import functools

import jax
import jax.numpy as jnp
from jax import lax
from jax.experimental import pallas as pl
from jax.experimental.pallas import tpu as pltpu
from jax.sharding import PartitionSpec as P

BF = jnp.bfloat16
F32 = jnp.float32
VMEM_LIMIT = 48 * 1024 * 1024
WHOLE = pl.BlockSpec(memory_space=pltpu.VMEM)
SCALARS = pl.BlockSpec(memory_space=pltpu.SMEM)


def swap(block, axis, offset):
    count = lax.axis_size(axis)
    return lax.ppermute(block, axis, [(i, i ^ offset) for i in range(count)])


def doubled(blocks, axis, offsets):
    for offset in offsets:
        blocks = blocks + [swap(block, axis, offset) for block in blocks]
    return blocks


def call(kernel, out_shape, count, flops, moved, **more):
    return pl.pallas_call(
        kernel,
        out_shape=out_shape,
        in_specs=more.pop("in_specs", [WHOLE] * count),
        compiler_params=pltpu.CompilerParams(vmem_limit_bytes=VMEM_LIMIT),
        cost_estimate=pl.CostEstimate(flops=flops, bytes_accessed=moved, transcendentals=0),
        **more,
    )


def onehot_kernel(ids_ref, out_ref):
    rows = lax.broadcasted_iota(jnp.int32, out_ref.shape, 0)
    out_ref[...] = (rows == ids_ref[...]).astype(F32).astype(BF)


def embed_kernel(onehot_ref, table_ref, out_ref):
    tokens = out_ref.shape[0]
    halo = onehot_ref.shape[1] - tokens
    out_ref[...] = lax.dot_general(
        onehot_ref[:, halo:], table_ref[...], (((0,), (0,)), ((), ())), preferred_element_type=F32
    ).astype(BF)


def band_kernel(filter_ref, out_ref):
    groups, taps = filter_ref.shape
    row = lax.broadcasted_iota(jnp.int32, (taps, taps), 0)
    col = lax.broadcasted_iota(jnp.int32, (taps, taps), 1)
    for g in range(groups):
        line = jnp.broadcast_to(filter_ref[g : g + 1, :].astype(F32), (taps, taps))
        ring = pltpu.roll(line, 0, 1, stride=1, stride_axis=0)
        out_ref[g, :taps, :] = jnp.where(col < row, ring, 0.0).astype(BF)
        out_ref[g, taps:, :] = jnp.where(col >= row, ring, 0.0).astype(BF)


def norm_kernel(where_ref, gain_ref, *refs):
    blocks, out_ref = refs[:-1], refs[-1]
    total = 0.0
    for block in blocks:
        wide = block[...].astype(F32)
        total = total + jnp.sum(wide * wide, axis=1, keepdims=True)
    scale = lax.rsqrt(total / (len(blocks) * blocks[0].shape[1]) + 1e-06)
    for j, block in enumerate(blocks):
        gain = gain_ref[where_ref[1] ^ j]
        out_ref[j] = (block[...].astype(F32) * scale * gain).astype(BF)


def project_kernel(where_ref, weight_ref, normed_ref, out_ref):
    pieces, _, depth = weight_ref.shape
    blocks = normed_ref.shape[0]
    each = pieces // blocks
    total = jnp.zeros(out_ref.shape, F32)
    for j in range(blocks):
        for r in range(each):
            total = total + lax.dot_general(
                weight_ref[(where_ref[1] ^ j) * each + r],
                normed_ref[j, :, r * depth : (r + 1) * depth],
                (((1,), (1,)), ((), ())),
                preferred_element_type=F32,
            )
    out_ref[...] = total.astype(BF)


def mixer_kernel(
    group_size, short_taps, where_ref, onehot_ref, param_ref, band_ref, *refs
):
    pieces, out_ref, proj_ref, gate_ref = refs[:-3], refs[-3], refs[-2], refs[-1]
    tokens = out_ref.shape[0]
    taps = band_ref.shape[2]
    length = onehot_ref.shape[1]
    halo = length - tokens
    width = pieces[0].shape[0] // 3
    inner = width // group_size
    blocks = tokens // taps
    for p, piece in enumerate(pieces):
        place = (where_ref[0] & (len(pieces) - 1)) ^ p
        proj_ref[...] = jnp.dot(piece[...], onehot_ref[...], preferred_element_type=F32)
        for g in range(inner):
            lower = g * group_size

            def taken(s):
                rows = pl.ds(s * width + lower, group_size)
                line = proj_ref[rows, :]
                factors = param_ref[place, rows, :]
                total = factors[:, 0:1] * line
                for lag in range(1, short_taps):
                    total = total + factors[:, lag : lag + 1] * pltpu.roll(line, lag, 1)
                return total

            product = (taken(1) * taken(2))[:, halo - taps :].astype(BF)
            stacked = jnp.concatenate(
                [product[:, b * taps : (b + 2) * taps] for b in range(blocks)], axis=0
            )
            mixed = jnp.dot(
                stacked, band_ref[place * inner + g], preferred_element_type=F32
            )
            conv = jnp.concatenate(
                [mixed[b * group_size : (b + 1) * group_size] for b in range(blocks)], axis=1
            )
            skip = param_ref[place, pl.ds(lower, group_size), :][:, short_taps : short_taps + 1]
            conv = conv + skip * product[:, taps:].astype(F32)
            gated = taken(0)[:, halo:] * conv
            begin = pl.multiple_of(place * width + lower, group_size)
            gate_ref[pl.ds(begin, group_size), :] = gated
    out_ref[...] = gate_ref[...].T.astype(BF)


def out_kernel(chunks, half, where_ref, *refs):
    gates, weights, out_ref, lhs_ref = refs[: 2 * chunks], refs[2 * chunks : -2], refs[-2], refs[-1]
    lane = gates[0].shape[1]
    depth = chunks * lane
    for side in range(2):
        for m in range(chunks):
            begin = pl.multiple_of(side * depth + (where_ref[2] ^ m) * lane, lane)
            lhs_ref[:, pl.ds(begin, lane)] = gates[side * chunks + m][...]
    weight = weights[0]
    count, cols = weight.shape[0] // 2, weight.shape[2]
    tokens = out_ref.shape[0]
    rows = min(tokens, 256)
    for b in range(count):
        place = ((where_ref[3] ^ half) * count + b) ^ where_ref[4]
        for begin in range(0, tokens, rows):
            out_ref[begin : begin + rows, b * cols : (b + 1) * cols] = jnp.dot(
                lhs_ref[begin : begin + rows, :], weight[place], preferred_element_type=F32
            ).astype(out_ref.dtype)


def final_kernel(embed_ref, own_ref, other_ref, out_ref):
    out_ref[...] = (
        embed_ref[...].astype(F32) + own_ref[...] + other_ref[...].astype(F32)
    ).astype(BF)


def body(
    token_ids, embed_table, norm_gain, in_weight, short_filter, long_filter, long_skip, out_weight
):
    seq, tp = lax.axis_index("seq"), lax.axis_index("tp")
    n, m = lax.axis_size("seq"), lax.axis_size("tp")
    tokens = token_ids.shape[0]
    vocab, width = embed_table.shape
    depth = in_weight.shape[0]
    groups, taps = long_filter.shape
    short_taps = short_filter.shape[0]
    piece = width // n
    chunks = 4
    per_chunk = n // chunks
    halo = 2 * taps
    top = n // 2
    upper = (seq >= top).astype(jnp.int32)
    core, row = tp & 1, tp >> 1

    weight = in_weight.reshape(depth, 3, n, piece).transpose(2, 1, 3, 0).reshape(n, 3 * piece, depth)
    weight = lax.all_to_all(weight, "seq", split_axis=0, concat_axis=0, tiled=True)

    table_row = swap(embed_table, "tp", 2)
    table_core = swap(embed_table, "tp", 1)
    table_both = swap(table_row, "tp", 1)

    tail = lax.ppermute(token_ids[tokens - halo :], "seq", [(i, i + 1) for i in range(n - 1)])
    tail = jnp.where(seq == 0, -1, tail)
    ids = jnp.concatenate([tail, token_ids])[None, :]
    length = tokens + halo

    chunk_at = (seq // per_chunk).astype(jnp.int32)
    same_side = row == upper
    base = jnp.where(same_side, seq, seq ^ top) & (top - 1)
    where = jnp.stack([seq, tp, chunk_at, core, base]).astype(jnp.int32)

    onehot = call(
        onehot_kernel, jax.ShapeDtypeStruct((vocab, length), BF), 1, vocab * length, 2 * vocab * length
    )(ids)
    embedded = call(
        embed_kernel,
        jax.ShapeDtypeStruct((tokens, width), BF),
        2,
        2 * tokens * vocab * width,
        2 * tokens * (vocab + width),
    )(onehot, embed_table)
    bands = call(
        band_kernel,
        jax.ShapeDtypeStruct((groups, 2 * taps, taps), BF),
        1,
        groups * taps * taps * 8,
        groups * taps * taps * 4,
    )(long_filter)
    params = short_filter.reshape(short_taps, 3, n, piece).transpose(2, 1, 3, 0)
    skips = jnp.broadcast_to(long_skip.reshape(n, 1, piece, 1), (n, 3, piece, 1))
    params = jnp.concatenate([params, skips], axis=3).reshape(n, 3 * piece, short_taps + 1)

    normed = call(
        norm_kernel,
        jax.ShapeDtypeStruct((m, vocab, width), BF),
        6,
        8 * m * vocab * width,
        4 * m * vocab * width,
        in_specs=[SCALARS] + [WHOLE] * 5,
    )(where, norm_gain.reshape(m, 1, width), embed_table, table_core, table_row, table_both)

    projected = call(
        project_kernel,
        jax.ShapeDtypeStruct((3 * piece, vocab), BF),
        3,
        2 * 3 * piece * vocab * m * width,
        2 * m * width * (vocab + 3 * piece),
        in_specs=[SCALARS, WHOLE, WHOLE],
    )(where, weight, normed)

    low = []
    bit = 1
    while bit < per_chunk:
        low.append(bit)
        bit *= 2
    first = projected
    second = swap(first, "seq", per_chunk)
    third = swap(first, "seq", 2 * per_chunk)
    fourth = swap(third, "seq", per_chunk)

    gates, row_gates = [], []
    chunk_width = per_chunk * piece
    mixer = functools.partial(mixer_kernel, width // groups, short_taps)
    for index, start in enumerate((first, second, third, fourth)):
        pieces = doubled([start], "seq", low)
        at = jnp.stack([seq, chunk_at ^ index]).astype(jnp.int32)
        inner = chunk_width * groups // width
        gate = pl.pallas_call(
            mixer,
            grid_spec=pltpu.PrefetchScalarGridSpec(
                num_scalar_prefetch=1,
                grid=(1,),
                in_specs=[
                    pl.BlockSpec((vocab, length), lambda i, s: (0, 0)),
                    pl.BlockSpec((per_chunk, 3 * piece, short_taps + 1), lambda i, s: (s[1], 0, 0)),
                    pl.BlockSpec((inner, 2 * taps, taps), lambda i, s: (s[1], 0, 0)),
                ]
                + [pl.BlockSpec((3 * piece, vocab), lambda i, s: (0, 0))] * len(pieces),
                out_specs=pl.BlockSpec((tokens, chunk_width), lambda i, s: (0, 0)),
                scratch_shapes=[
                    pltpu.VMEM((3 * piece, length), F32),
                    pltpu.VMEM((chunk_width, tokens), F32),
                ],
            ),
            out_shape=jax.ShapeDtypeStruct((tokens, chunk_width), BF),
            compiler_params=pltpu.CompilerParams(vmem_limit_bytes=VMEM_LIMIT),
            cost_estimate=pl.CostEstimate(
                flops=2 * 3 * chunk_width * length * vocab,
                bytes_accessed=4 * vocab * length,
                transcendentals=0,
            ),
        )(at, onehot, params, bands, *pieces)
        gates.append(gate)
        row_gates.append(swap(gate, "tp", 2))

    mids = []
    bit = 2
    while bit < top:
        mids.append(bit)
        bit *= 2
    near = doubled([out_weight], "seq", mids)
    far = doubled([swap(out_weight, "seq", top)], "seq", mids)
    near, far = jnp.stack(near), jnp.stack(far)
    kept = jnp.where(same_side, near, far)
    given = swap(jnp.where(same_side, far, near), "tp", 2)
    both = jnp.concatenate([kept, given], axis=1)
    across = swap(both, "seq", 1)
    columns = jnp.stack([both, across], axis=1).reshape(top, 2 * width, out_weight.shape[1])

    def out_part(half, kind):
        count = 2 * chunks
        return call(
            functools.partial(out_kernel, chunks, half),
            jax.ShapeDtypeStruct((tokens, width), kind),
            count + 2,
            2 * tokens * 2 * width * width,
            4 * tokens * width + 4 * width * width,
            in_specs=[SCALARS] + [WHOLE] * (count + 1),
            scratch_shapes=[pltpu.VMEM((tokens, 2 * width), BF)],
        )(where, *gates, *row_gates, columns)

    sent = swap(out_part(1, BF), "tp", 1)
    own = out_part(0, F32)
    return call(
        final_kernel,
        jax.ShapeDtypeStruct((tokens, width), BF),
        3,
        2 * tokens * width,
        8 * tokens * width,
    )(embedded, own, sent)


def solution(mesh):
    placed = (
        P("seq"),
        P(None, "tp"),
        P(),
        P("seq", None, "tp"),
        P(None, None, "tp"),
        P("tp", None),
        P("tp"),
        P("tp", "seq"),
    )
    return jax.shard_map(
        body, mesh=mesh, in_specs=placed, out_specs=P("seq", "tp"), check_vma=False
    )
```

```python
import functools

import jax
import jax.numpy as jnp
from jax import lax
from jax.experimental import pallas as pl
from jax.experimental.pallas import tpu as pltpu
from jax.sharding import PartitionSpec as P

BF = jnp.bfloat16
F32 = jnp.float32
MIB = 1024 * 1024
WHOLE = pl.BlockSpec(memory_space=pltpu.VMEM)
SCALARS = pl.BlockSpec(memory_space=pltpu.SMEM)


def swap(block, axis, offset):
    count = lax.axis_size(axis)
    return lax.ppermute(block, axis, [(i, i ^ offset) for i in range(count)])


def cost_us(time):
    return int(time * 1.1e9)


def call(kernel, out_shape, count, flops, moved, room=12, **more):
    return pl.pallas_call(
        kernel,
        out_shape=out_shape,
        in_specs=more.pop("in_specs", [WHOLE] * count),
        compiler_params=pltpu.CompilerParams(vmem_limit_bytes=room * MIB),
        cost_estimate=pl.CostEstimate(flops=flops, bytes_accessed=moved, transcendentals=0),
        **more,
    )


def after(value, *earlier):
    return lax.optimization_barrier((value, earlier))[0]


def turn_kernel(where_ref, weight_ref, *refs):
    out_refs, turned_ref = refs[:-1], refs[-1]
    top = len(out_refs)
    rows = out_refs[0].shape[1]
    piece = rows // 3
    for s in range(3):
        turned_ref[...] = weight_ref[s].astype(F32).T.astype(BF).reshape(turned_ref.shape)
        for offset, out_ref in enumerate(out_refs):
            for far in range(2):
                place = where_ref[0] ^ (offset + far * top)
                out_ref[far, s * piece : (s + 1) * piece, :] = turned_ref[place]


def onehot(ids, vocab):
    entries = lax.broadcasted_iota(jnp.int32, (ids.shape[0], vocab), 1)
    return (entries == ids).astype(F32).astype(BF)


def embed_kernel(ids_ref, table_ref, out_ref):
    halo = ids_ref.shape[0] - out_ref.shape[0]
    out_ref[...] = jnp.dot(
        onehot(ids_ref[halo:, :], table_ref.shape[0]), table_ref[...], preferred_element_type=F32
    ).astype(BF)


def band_kernel(filter_ref, out_ref):
    groups, taps = filter_ref.shape
    row = lax.broadcasted_iota(jnp.int32, (taps, taps), 0)
    col = lax.broadcasted_iota(jnp.int32, (taps, taps), 1)
    for g in range(groups):
        line = jnp.broadcast_to(filter_ref[g : g + 1, :].astype(F32), (taps, taps))
        ring = pltpu.roll(line, 0, 1, stride=1, stride_axis=0)
        out_ref[g, :taps, :] = jnp.where(col < row, ring, 0.0).astype(BF)
        out_ref[g, taps:, :] = jnp.where(col >= row, ring, 0.0).astype(BF)


def norm_kernel(where_ref, gain_ref, *refs):
    blocks, out_ref, kept_ref, sem = refs[:-3], refs[-3], refs[-2], refs[-1]
    pieces, _, depth = out_ref.shape
    each = pieces // len(blocks)
    total = 0.0
    for block in blocks:
        wide = block[...].astype(F32)
        total = total + jnp.sum(wide * wide, axis=1, keepdims=True)
    scale = lax.rsqrt(total / (len(blocks) * blocks[0].shape[1]) + 1e-06)
    for j, block in enumerate(blocks):
        place = where_ref[1] ^ j
        result = (block[...].astype(F32) * scale * gain_ref[place]).astype(BF)
        for r in range(each):
            kept_ref[place * each + r] = result[:, r * depth : (r + 1) * depth]
    copy = pltpu.make_async_copy(kept_ref, out_ref, sem)
    copy.start()
    copy.wait()


def project_kernel(where_ref, normed_ref, crossing_ref, *refs):
    parts, out_ref, kept_ref, sem = refs[:-3], refs[-3], refs[-2], refs[-1]
    top = len(parts)
    copy = pltpu.make_async_copy(normed_ref, kept_ref, sem)
    copy.start()
    copy.wait()
    total = jnp.zeros(out_ref.shape, F32)
    for offset in range(2 * top):
        weight = parts[offset][0] if offset < top else crossing_ref[offset - top]
        total = total + lax.dot_general(
            weight,
            kept_ref[where_ref[0] ^ offset],
            (((1,), (1,)), ((), ())),
            preferred_element_type=F32,
        )
    out_ref[...] = total.astype(BF)


def mixer_kernel(
    group_size, where_ref, ids_ref, short_ref, skip_ref, band_ref, *refs
):
    pieces = refs[:-6]
    out_ref, rows_ref, proj_ref, product_ref, turned_ref, conv_ref = refs[-6:]
    tokens, width = out_ref.shape
    short_taps = short_ref.shape[0]
    taps = band_ref.shape[2]
    length, vocab = ids_ref.shape[0], rows_ref.shape[1]
    halo = length - tokens
    piece = width // len(pieces)
    blocks = tokens // taps
    for p, block in enumerate(pieces):
        place = (where_ref[0] & (len(pieces) - 1)) ^ p
        for s in range(3):
            begin = pl.multiple_of(s * width + place * piece, piece)
            rows_ref[pl.ds(begin, piece), :] = block[s * piece : (s + 1) * piece, :]
    step = 2 * taps
    for begin in range(0, length, step):
        count = min(step, length - begin)
        result = lax.dot_general(
            onehot(ids_ref[begin : begin + count, :], vocab),
            rows_ref[...],
            (((1,), (1,)), ((), ())),
            preferred_element_type=F32,
        )
        for s in range(3):
            proj_ref[s, begin : begin + count, :] = result[:, s * width : (s + 1) * width]

    def taken(s, begin):
        total = short_ref[0, s : s + 1, :] * proj_ref[s, begin : begin + taps, :]
        for lag in range(1, short_taps):
            total = total + short_ref[lag, s : s + 1, :] * proj_ref[s, begin - lag : begin - lag + taps, :]
        return total

    for b in range(blocks + 1):
        begin = halo + (b - 1) * taps
        product = (taken(1, begin) * taken(2, begin)).astype(BF).astype(F32)
        product_ref[b * taps : (b + 1) * taps, :] = product
        turned_ref[:, b * taps : (b + 1) * taps] = product.T.astype(BF)
    for g in range(width // group_size):
        rows = slice(g * group_size, (g + 1) * group_size)
        stacked = jnp.concatenate(
            [turned_ref[rows, b * taps : (b + 2) * taps] for b in range(blocks)], axis=0
        )
        mixed = jnp.dot(stacked, band_ref[g], preferred_element_type=F32)
        for b in range(blocks):
            conv_ref[rows, b * taps : (b + 1) * taps] = mixed[b * group_size : (b + 1) * group_size]
    for b in range(blocks):
        conv = conv_ref[:, b * taps : (b + 1) * taps].T
        conv = conv + skip_ref[...] * product_ref[(b + 1) * taps : (b + 2) * taps, :]
        gated = taken(0, halo + b * taps) * conv
        out_ref[b * taps : (b + 1) * taps, :] = gated.astype(BF)


def most_kernel(chunks, where_ref, *refs):
    count = 2 * chunks - 1
    gates, weights, out_ref, last_ref, lhs_ref, rhs_ref = (
        refs[:count], refs[count:-4], refs[-4], refs[-3], refs[-2], refs[-1]
    )
    tokens, lane = gates[0].shape
    width = chunks * lane
    top, _, cols = rhs_ref.shape
    for index, weight in enumerate(weights):
        offset, side = index // 2, index % 2
        rhs_ref[offset ^ where_ref[4], side * width : (side + 1) * width, :] = weight[...]
    for index, gate in enumerate(gates):
        side, m = index // chunks, index % chunks
        begin = pl.multiple_of(side * width + (where_ref[2] ^ m) * lane, lane)
        lhs_ref[:, pl.ds(begin, lane)] = gate[...]
    missing = pl.multiple_of(width + (where_ref[2] ^ (chunks - 1)) * lane, lane)
    lhs_ref[:, pl.ds(missing, lane)] = jnp.zeros((tokens, lane), BF)
    rows = min(tokens, 256)
    for half in range(2):
        for b in range(top // 2):
            place = (where_ref[3] ^ half) * (top // 2) + b
            at = slice(b * cols, (b + 1) * cols)
            last_ref[half, :, at] = rhs_ref[place, pl.ds(missing, lane), :]
            for begin in range(0, tokens, rows):
                out_ref[half, begin : begin + rows, at] = jnp.dot(
                    lhs_ref[begin : begin + rows, :], rhs_ref[place], preferred_element_type=F32
                )


def sent_kernel(most_ref, gate_ref, weight_ref, out_ref):
    out_ref[...] = (
        most_ref[0] + jnp.dot(gate_ref[...], weight_ref[0], preferred_element_type=F32)
    ).astype(BF)


def final_kernel(most_ref, gate_ref, weight_ref, embed_ref, other_ref, out_ref):
    own = most_ref[0] + jnp.dot(gate_ref[...], weight_ref[0], preferred_element_type=F32)
    out_ref[...] = (embed_ref[...].astype(F32) + own + other_ref[...].astype(F32)).astype(BF)


def body(
    token_ids, embed_table, norm_gain, in_weight, short_filter, long_filter, long_skip, out_weight
):
    chunks = 4
    n, minor = 2 * chunks, lax.axis_size("seq") // (2 * chunks)
    device, tp, m = lax.axis_index("seq"), lax.axis_index("tp"), lax.axis_size("tp")
    seq = device // minor
    tokens = token_ids.shape[0]
    vocab, width = embed_table.shape
    groups, taps = long_filter.shape
    short_taps = short_filter.shape[0]
    piece = width // n
    per_chunk = n // chunks
    lane = per_chunk * piece
    halo = taps + 16 * -(-(short_taps - 1) // 16)
    length = tokens + halo
    top = n // 2
    upper = (seq >= top).astype(jnp.int32)
    core, row = tp & 1, tp >> 1
    same_side = row == upper
    chunk_at = seq // per_chunk
    where = jnp.stack([seq, tp, chunk_at, core, seq & (top - 1)]).astype(jnp.int32)

    def over(block, offset):
        return swap(block, "seq", offset * minor)

    if minor > 1:
        parts = [[g * minor + j for j in range(minor)] for g in range(n)]
        in_weight = lax.all_gather(in_weight, "seq", axis=0, tiled=True, axis_index_groups=parts)
        out_weight = lax.all_gather(out_weight, "seq", axis=1, tiled=True, axis_index_groups=parts)
    depth = in_weight.shape[0]

    near = [out_weight]
    far = [over(out_weight, top)]

    parts = call(
        turn_kernel,
        [jax.ShapeDtypeStruct((2, 3 * piece, depth), BF)] * top,
        2,
        cost_us(1.0),
        4 * 3 * width * depth,
        in_specs=[SCALARS, WHOLE],
        scratch_shapes=[pltpu.VMEM((n, piece, depth), BF)],
    )(where, in_weight.transpose(1, 0, 2))
    parts = [over(part, offset) if offset else part for offset, part in enumerate(parts)]

    table_row = swap(embed_table, "tp", 2)
    table_core = swap(embed_table, "tp", 1)
    table_both = swap(table_row, "tp", 1)

    crossing = after(jnp.stack([part[1] for part in parts]), far[0], table_row, table_core)
    crossing = over(crossing, top)

    tail = lax.ppermute(token_ids[tokens - halo :], "seq", [(i, i + 1) for i in range(n * minor - 1)])
    tail = jnp.where(device == 0, -1, tail)
    ids = jnp.concatenate([tail, token_ids])[:, None]

    embedded = call(
        embed_kernel, jax.ShapeDtypeStruct((tokens, width), BF), 2, cost_us(1.0), 2 * tokens * width
    )(ids, embed_table)
    bands = call(
        band_kernel, jax.ShapeDtypeStruct((groups, 2 * taps, taps), BF), 1, cost_us(0.5), groups * taps
    )(long_filter)

    near.append(over(near[0], 2))
    far.append(over(far[0], 2))
    normed = call(
        norm_kernel,
        jax.ShapeDtypeStruct((n, vocab, depth), BF),
        6,
        cost_us(1.5),
        4 * m * vocab * width,
        in_specs=[SCALARS] + [WHOLE] * 5,
        out_specs=pl.BlockSpec(memory_space=pltpu.HBM),
        scratch_shapes=[pltpu.VMEM((n, vocab, depth), BF), pltpu.SemaphoreType.DMA],
    )(where, norm_gain.reshape(m, 1, width), embed_table, table_core, table_row, table_both)

    halves = []
    for one, two in zip(near, far, strict=True):
        kept = jnp.where(same_side, one, two)
        given = jnp.where(same_side, two, one)
        given = swap(given, "tp", 2)
        halves += [kept, given, over(kept, 1), over(given, 1)]

    projected = call(
        project_kernel,
        jax.ShapeDtypeStruct((3 * piece, vocab), BF),
        3,
        cost_us(2.0),
        2 * m * width * (vocab + 3 * piece),
        in_specs=[SCALARS, pl.BlockSpec(memory_space=pltpu.HBM)] + [WHOLE] * (top + 1),
        scratch_shapes=[pltpu.VMEM((n, vocab, depth), BF), pltpu.SemaphoreType.DMA],
    )(where, normed, crossing, *parts)

    starts = [projected, over(projected, 2), over(projected, top)]
    gates, row_gates = [], []
    for index in range(chunks):
        if index == 1:
            starts[2] = after(starts[2], gates[0])
            starts.append(over(starts[2], 2))
        pieces = [starts[index], over(starts[index], 1)]
        at = jnp.stack([seq, chunk_at ^ index]).astype(jnp.int32)
        if index == 0:
            at = after(at, *halves)
        gate = pl.pallas_call(
            functools.partial(mixer_kernel, width // groups),
            grid_spec=pltpu.PrefetchScalarGridSpec(
                num_scalar_prefetch=1,
                grid=(1,),
                in_specs=[
                    pl.BlockSpec((length, 1), lambda i, s: (0, 0)),
                    pl.BlockSpec((short_taps, 3, lane), lambda i, s: (0, 0, s[1])),
                    pl.BlockSpec((1, lane), lambda i, s: (0, s[1])),
                    pl.BlockSpec((lane * groups // width, 2 * taps, taps), lambda i, s: (s[1], 0, 0)),
                ]
                + [pl.BlockSpec((3 * piece, vocab), lambda i, s: (0, 0))] * len(pieces),
                out_specs=pl.BlockSpec((tokens, lane), lambda i, s: (0, 0)),
                scratch_shapes=[
                    pltpu.VMEM((3 * lane, vocab), BF),
                    pltpu.VMEM((3, length, lane), F32),
                    pltpu.VMEM((tokens + taps, lane), F32),
                    pltpu.VMEM((lane, tokens + taps), BF),
                    pltpu.VMEM((lane, tokens), F32),
                ],
            ),
            out_shape=jax.ShapeDtypeStruct((tokens, lane), BF),
            compiler_params=pltpu.CompilerParams(vmem_limit_bytes=12 * MIB),
            cost_estimate=pl.CostEstimate(
                flops=cost_us(3.5), bytes_accessed=4 * vocab * length, transcendentals=0
            ),
        )(at, ids, short_filter, long_skip[None, :], bands, *pieces)
        gates.append(gate)
        row_gates.append(swap(gate, "tp", 2))

    most, last = call(
        functools.partial(most_kernel, chunks),
        [
            jax.ShapeDtypeStruct((2, tokens, width), F32),
            jax.ShapeDtypeStruct((2, lane, width), BF),
        ],
        2 * chunks + 2 * top,
        cost_us(4.0),
        8 * tokens * width,
        room=24,
        in_specs=[SCALARS] + [WHOLE] * (2 * chunks - 1 + 2 * top),
        scratch_shapes=[
            pltpu.VMEM((tokens, 2 * width), BF),
            pltpu.VMEM((top, 2 * width, width * 2 // top), BF),
        ],
    )(where, *gates, *row_gates[:-1], *halves)

    def half_spec(shape, half):
        return pl.BlockSpec((1,) + shape, lambda i: (half, 0, 0))

    rows = tokens // 4
    def stepped(kernel, half, more):
        return pl.pallas_call(
            kernel,
            grid=(tokens // rows,),
            in_specs=[
                pl.BlockSpec((1, rows, width), lambda i: (half, i, 0)),
                pl.BlockSpec((rows, lane), lambda i: (i, 0)),
                pl.BlockSpec((1, lane, width), lambda i: (half, 0, 0)),
            ]
            + [pl.BlockSpec((rows, width), lambda i: (i, 0))] * more,
            out_specs=pl.BlockSpec((rows, width), lambda i: (i, 0)),
            out_shape=jax.ShapeDtypeStruct((tokens, width), BF),
            compiler_params=pltpu.CompilerParams(vmem_limit_bytes=12 * MIB),
            cost_estimate=pl.CostEstimate(
                flops=cost_us(1.5), bytes_accessed=8 * tokens * width, transcendentals=0
            ),
        )

    sent = swap(stepped(sent_kernel, 1, 0)(most, row_gates[-1], last), "tp", 1)
    return stepped(final_kernel, 0, 2)(most, row_gates[-1], last, embedded, sent)


def solution(mesh):
    placed = (
        P("seq"),
        P(None, "tp"),
        P(),
        P("seq", None, "tp"),
        P(None, None, "tp"),
        P("tp", None),
        P("tp"),
        P("tp", "seq"),
    )
    return jax.shard_map(
        body, mesh=mesh, in_specs=placed, out_specs=P("seq", "tp"), check_vma=False
    )
```

```python
import functools

import jax
import jax.numpy as jnp
from jax import lax
from jax.experimental import pallas as pl
from jax.experimental.pallas import tpu as pltpu
from jax.sharding import PartitionSpec as P

BF = jnp.bfloat16
F32 = jnp.float32
MIB = 1024 * 1024
WHOLE = pl.BlockSpec(memory_space=pltpu.VMEM)
SCALARS = pl.BlockSpec(memory_space=pltpu.SMEM)


def swap(block, axis, offset):
    count = lax.axis_size(axis)
    return lax.ppermute(block, axis, [(i, i ^ offset) for i in range(count)])


def cost_us(time):
    return int(time * 1.1e9)


def call(kernel, out_shape, count, flops, moved, room=12, **more):
    return pl.pallas_call(
        kernel,
        out_shape=out_shape,
        in_specs=more.pop("in_specs", [WHOLE] * count),
        compiler_params=pltpu.CompilerParams(vmem_limit_bytes=room * MIB),
        cost_estimate=pl.CostEstimate(flops=flops, bytes_accessed=moved, transcendentals=0),
        **more,
    )


def after(value, *earlier):
    return lax.optimization_barrier((value, earlier))[0]


def turn_kernel(where_ref, weight_ref, *refs):
    out_refs, (held_ref, turned_ref, sems) = refs[:-3], refs[-3:]
    top = len(out_refs)
    rows = out_refs[0].shape[1]
    piece = rows // 3
    copies = [
        pltpu.make_async_copy(weight_ref.at[s], held_ref.at[s], sems.at[s]) for s in range(3)
    ]
    for copy in copies:
        copy.start()
    for s, copy in enumerate(copies):
        copy.wait()
        turned_ref[...] = held_ref[s].astype(F32).T.astype(BF).reshape(turned_ref.shape)
        for offset, out_ref in enumerate(out_refs):
            for far in range(2):
                place = where_ref[0] ^ (offset + far * top)
                out_ref[far, s * piece : (s + 1) * piece, :] = turned_ref[place]


def onehot(ids, vocab):
    entries = lax.broadcasted_iota(jnp.int32, (ids.shape[0], vocab), 1)
    return (entries == ids).astype(F32).astype(BF)


def embed_kernel(ids_ref, table_ref, out_ref):
    halo = ids_ref.shape[0] - out_ref.shape[0]
    out_ref[...] = jnp.dot(
        onehot(ids_ref[halo:, :], table_ref.shape[0]), table_ref[...], preferred_element_type=F32
    ).astype(BF)


def band_kernel(filter_ref, out_ref):
    groups, taps = filter_ref.shape
    row = lax.broadcasted_iota(jnp.int32, (taps, taps), 0)
    col = lax.broadcasted_iota(jnp.int32, (taps, taps), 1)
    for g in range(groups):
        line = jnp.broadcast_to(filter_ref[g : g + 1, :].astype(F32), (taps, taps))
        ring = pltpu.roll(line, 0, 1, stride=1, stride_axis=0)
        out_ref[g, :taps, :] = jnp.where(col < row, ring, 0.0).astype(BF)
        out_ref[g, taps:, :] = jnp.where(col >= row, ring, 0.0).astype(BF)


def norm_kernel(where_ref, gain_ref, *refs):
    blocks, out_ref, kept_ref, sem = refs[:-3], refs[-3], refs[-2], refs[-1]
    pieces, _, depth = out_ref.shape
    each = pieces // len(blocks)
    total = 0.0
    for block in blocks:
        wide = block[...].astype(F32)
        total = total + jnp.sum(wide * wide, axis=1, keepdims=True)
    scale = lax.rsqrt(total / (len(blocks) * blocks[0].shape[1]) + 1e-06)
    for j, block in enumerate(blocks):
        place = where_ref[1] ^ j
        result = (block[...].astype(F32) * scale * gain_ref[place]).astype(BF)
        for r in range(each):
            kept_ref[place * each + r] = result[:, r * depth : (r + 1) * depth]
    copy = pltpu.make_async_copy(kept_ref, out_ref, sem)
    copy.start()
    copy.wait()


def project_kernel(where_ref, normed_ref, crossing_ref, *refs):
    parts, out_ref, kept_ref, sem = refs[:-3], refs[-3], refs[-2], refs[-1]
    top = len(parts)
    copy = pltpu.make_async_copy(normed_ref, kept_ref, sem)
    copy.start()
    copy.wait()
    total = jnp.zeros(out_ref.shape, F32)
    for offset in range(2 * top):
        weight = parts[offset][0] if offset < top else crossing_ref[offset - top]
        total = total + lax.dot_general(
            weight,
            kept_ref[where_ref[0] ^ offset],
            (((1,), (1,)), ((), ())),
            preferred_element_type=F32,
        )
    out_ref[...] = total.astype(BF)


def mixer_kernel(
    group_size, where_ref, ids_ref, short_ref, skip_ref, band_ref, *refs
):
    pieces = refs[:-6]
    out_ref, rows_ref, proj_ref, product_ref, turned_ref, conv_ref = refs[-6:]
    tokens, width = out_ref.shape
    short_taps = short_ref.shape[0]
    taps = band_ref.shape[2]
    length, vocab = ids_ref.shape[0], rows_ref.shape[1]
    halo = length - tokens
    piece = width // len(pieces)
    blocks = tokens // taps
    for p, block in enumerate(pieces):
        place = (where_ref[0] & (len(pieces) - 1)) ^ p
        for s in range(3):
            begin = pl.multiple_of(s * width + place * piece, piece)
            rows_ref[pl.ds(begin, piece), :] = block[s * piece : (s + 1) * piece, :]
    step = 2 * taps
    for begin in range(0, length, step):
        count = min(step, length - begin)
        result = lax.dot_general(
            onehot(ids_ref[begin : begin + count, :], vocab),
            rows_ref[...],
            (((1,), (1,)), ((), ())),
            preferred_element_type=F32,
        )
        for s in range(3):
            proj_ref[s, begin : begin + count, :] = result[:, s * width : (s + 1) * width]

    def taken(s, begin):
        total = short_ref[0, s : s + 1, :] * proj_ref[s, begin : begin + taps, :]
        for lag in range(1, short_taps):
            total = total + short_ref[lag, s : s + 1, :] * proj_ref[s, begin - lag : begin - lag + taps, :]
        return total

    for b in range(blocks + 1):
        begin = halo + (b - 1) * taps
        product = (taken(1, begin) * taken(2, begin)).astype(BF).astype(F32)
        product_ref[b * taps : (b + 1) * taps, :] = product
        turned_ref[:, b * taps : (b + 1) * taps] = product.T.astype(BF)
    for g in range(width // group_size):
        rows = slice(g * group_size, (g + 1) * group_size)
        stacked = jnp.concatenate(
            [turned_ref[rows, b * taps : (b + 2) * taps] for b in range(blocks)], axis=0
        )
        mixed = jnp.dot(stacked, band_ref[g], preferred_element_type=F32)
        for b in range(blocks):
            conv_ref[rows, b * taps : (b + 1) * taps] = mixed[b * group_size : (b + 1) * group_size]
    for b in range(blocks):
        conv = conv_ref[:, b * taps : (b + 1) * taps].T
        conv = conv + skip_ref[...] * product_ref[(b + 1) * taps : (b + 2) * taps, :]
        gated = taken(0, halo + b * taps) * conv
        out_ref[b * taps : (b + 1) * taps, :] = gated.astype(BF)


def most_kernel(chunks, late, where_ref, *refs):
    count = 2 * chunks - late
    gates, weights, (out_ref, last_ref, lhs_ref, rhs_ref) = refs[:count], refs[count:-4], refs[-4:]
    tokens, lane = gates[0].shape
    width = chunks * lane
    top, _, cols = rhs_ref.shape
    for index, weight in enumerate(weights):
        offset, side = index // 2, index % 2
        rhs_ref[offset ^ where_ref[4], side * width : (side + 1) * width, :] = weight[...]
    for index in range(2 * chunks):
        side, m = index // chunks, index % chunks
        begin = pl.multiple_of(side * width + (where_ref[2] ^ m) * lane, lane)
        if index < count:
            lhs_ref[:, pl.ds(begin, lane)] = gates[index][...]
        else:
            lhs_ref[:, pl.ds(begin, lane)] = jnp.zeros((tokens, lane), BF)
    rows = min(tokens, 256)
    for half in range(2):
        for b in range(top // 2):
            place = (where_ref[3] ^ half) * (top // 2) + b
            at = slice(b * cols, (b + 1) * cols)
            for late_index in range(late):
                begin = width + (where_ref[2] ^ (chunks - late + late_index)) * lane
                last_ref[half, late_index * lane : (late_index + 1) * lane, at] = rhs_ref[
                    place, pl.ds(pl.multiple_of(begin, lane), lane), :
                ]
            for begin in range(0, tokens, rows):
                out_ref[half, begin : begin + rows, at] = jnp.dot(
                    lhs_ref[begin : begin + rows, :], rhs_ref[place], preferred_element_type=F32
                ).astype(out_ref.dtype)


def with_late(most_ref, weight_ref, gates):
    total = most_ref[0].astype(F32)
    lane = gates[0].shape[1]
    for index, gate in enumerate(gates):
        weight = weight_ref[0, index * lane : (index + 1) * lane, :]
        total = total + jnp.dot(gate[...], weight, preferred_element_type=F32)
    return total


def sent_kernel(most_ref, weight_ref, *refs):
    gates, out_ref = refs[:-1], refs[-1]
    out_ref[...] = with_late(most_ref, weight_ref, gates).astype(BF)


def final_kernel(most_ref, weight_ref, *refs):
    gates, (embed_ref, other_ref, out_ref) = refs[:-3], refs[-3:]
    own = with_late(most_ref, weight_ref, gates)
    out_ref[...] = (embed_ref[...].astype(F32) + own + other_ref[...].astype(F32)).astype(BF)


def body(
    token_ids, embed_table, norm_gain, in_weight, short_filter, long_filter, long_skip, out_weight
):
    chunks = 4
    n, minor = 2 * chunks, lax.axis_size("seq") // (2 * chunks)
    device, tp, m = lax.axis_index("seq"), lax.axis_index("tp"), lax.axis_size("tp")
    seq = device // minor
    tokens = token_ids.shape[0]
    vocab, width = embed_table.shape
    groups, taps = long_filter.shape
    short_taps = short_filter.shape[0]
    piece = width // n
    per_chunk = n // chunks
    lane = per_chunk * piece
    halo = taps + 16 * -(-(short_taps - 1) // 16)
    length = tokens + halo
    top = n // 2
    upper = (seq >= top).astype(jnp.int32)
    core, row = tp & 1, tp >> 1
    same_side = row == upper
    chunk_at = seq // per_chunk
    where = jnp.stack([seq, tp, chunk_at, core, seq & (top - 1)]).astype(jnp.int32)

    def over(block, offset):
        return swap(block, "seq", offset * minor)

    if minor > 1:
        parts = [[g * minor + j for j in range(minor)] for g in range(n)]
        in_weight = lax.all_gather(in_weight, "seq", axis=0, tiled=True, axis_index_groups=parts)
        out_weight = lax.all_gather(out_weight, "seq", axis=1, tiled=True, axis_index_groups=parts)
    depth = in_weight.shape[0]

    near = [out_weight]
    far = [over(out_weight, top)]

    parts = call(
        turn_kernel,
        [jax.ShapeDtypeStruct((2, 3 * piece, depth), BF)] * top,
        2,
        cost_us(1.0),
        4 * 3 * width * depth,
        in_specs=[SCALARS, pl.BlockSpec(memory_space=pltpu.HBM)],
        scratch_shapes=[
            pltpu.VMEM((3, depth, width), BF),
            pltpu.VMEM((n, piece, depth), BF),
            pltpu.SemaphoreType.DMA((3,)),
        ],
    )(where, in_weight.transpose(1, 0, 2))
    parts = [over(part, offset) if offset else part for offset, part in enumerate(parts)]

    table_row = swap(embed_table, "tp", 2)
    table_core = swap(embed_table, "tp", 1)
    table_both = swap(table_row, "tp", 1)

    crossing = after(jnp.stack([part[1] for part in parts]), far[0], table_row, table_core)
    crossing = over(crossing, top)

    bands = call(
        band_kernel, jax.ShapeDtypeStruct((groups, 2 * taps, taps), BF), 1, cost_us(0.5), groups * taps
    )(long_filter)

    tail = lax.ppermute(after(token_ids, table_both)[tokens - halo :], "seq", [(i, i + 1) for i in range(n * minor - 1)])
    tail = jnp.where(device == 0, -1, tail)
    ids = jnp.concatenate([tail, token_ids])[:, None]

    near.append(over(near[0], 2))
    far.append(over(far[0], 2))
    normed = call(
        norm_kernel,
        jax.ShapeDtypeStruct((n, vocab, depth), BF),
        6,
        cost_us(1.5),
        4 * m * vocab * width,
        in_specs=[SCALARS] + [WHOLE] * 5,
        out_specs=pl.BlockSpec(memory_space=pltpu.HBM),
        scratch_shapes=[pltpu.VMEM((n, vocab, depth), BF), pltpu.SemaphoreType.DMA],
    )(where, norm_gain.reshape(m, 1, width), embed_table, table_core, table_row, table_both)

    halves = []
    for one, two in zip(near, far, strict=True):
        kept = jnp.where(same_side, one, two)
        given = jnp.where(same_side, two, one)
        given = swap(given, "tp", 2)
        halves += [kept, given, over(kept, 1), over(given, 1)]

    parts[0] = after(parts[0], ids)
    projected = call(
        project_kernel,
        jax.ShapeDtypeStruct((3 * piece, vocab), BF),
        3,
        cost_us(10.0),
        2 * m * width * (vocab + 3 * piece),
        in_specs=[SCALARS, pl.BlockSpec(memory_space=pltpu.HBM)] + [WHOLE] * (top + 1),
        scratch_shapes=[pltpu.VMEM((n, vocab, depth), BF), pltpu.SemaphoreType.DMA],
    )(where, normed, crossing, *parts)

    embedded = call(
        embed_kernel, jax.ShapeDtypeStruct((tokens, width), BF), 2, cost_us(1.0), 2 * tokens * width
    )(ids, embed_table)
    halves[-1] = over(after(halves[-3], projected), 1)
    starts = [projected, over(projected, 2), over(projected, top)]
    gates, row_gates, besides = [], [], []
    for index in range(chunks):
        if index == 1:
            starts[2] = after(starts[2], gates[0])
            starts.append(over(starts[2], 2))
        pieces = [starts[index], over(starts[index], 1) if index < 3 else over(besides[2], 2)]
        besides.append(pieces[1])
        at = jnp.stack([seq, chunk_at ^ index]).astype(jnp.int32)
        if index == 2:
            at = after(at, row_gates[0])
        if index == 0:
            at = after(at, *halves[:-1])
        gate = pl.pallas_call(
            functools.partial(mixer_kernel, width // groups),
            grid_spec=pltpu.PrefetchScalarGridSpec(
                num_scalar_prefetch=1,
                grid=(1,),
                in_specs=[
                    pl.BlockSpec((length, 1), lambda i, s: (0, 0)),
                    pl.BlockSpec((short_taps, 3, lane), lambda i, s: (0, 0, s[1])),
                    pl.BlockSpec((1, lane), lambda i, s: (0, s[1])),
                    pl.BlockSpec((lane * groups // width, 2 * taps, taps), lambda i, s: (s[1], 0, 0)),
                ]
                + [pl.BlockSpec((3 * piece, vocab), lambda i, s: (0, 0))] * len(pieces),
                out_specs=pl.BlockSpec((tokens, lane), lambda i, s: (0, 0)),
                scratch_shapes=[
                    pltpu.VMEM((3 * lane, vocab), BF),
                    pltpu.VMEM((3, length, lane), F32),
                    pltpu.VMEM((tokens + taps, lane), F32),
                    pltpu.VMEM((lane, tokens + taps), BF),
                    pltpu.VMEM((lane, tokens), F32),
                ],
            ),
            out_shape=jax.ShapeDtypeStruct((tokens, lane), BF),
            compiler_params=pltpu.CompilerParams(vmem_limit_bytes=12 * MIB),
            cost_estimate=pl.CostEstimate(
                flops=cost_us(3.5), bytes_accessed=4 * vocab * length, transcendentals=0
            ),
        )(at, ids, short_filter, long_skip[None, :], bands, *pieces)
        gates.append(gate)
        row_gates.append(swap(gate, "tp", 2))

    late = 2
    most, last = call(
        functools.partial(most_kernel, chunks, late),
        [
            jax.ShapeDtypeStruct((2, tokens, width), BF),
            jax.ShapeDtypeStruct((2, late * lane, width), BF),
        ],
        0,
        cost_us(4.0),
        8 * tokens * width,
        room=24,
        in_specs=[SCALARS] + [WHOLE] * (2 * chunks - late + 2 * top),
        scratch_shapes=[
            pltpu.VMEM((tokens, 2 * width), BF),
            pltpu.VMEM((top, 2 * width, width * 2 // top), BF),
        ],
    )(where, *gates, *row_gates[:-late], *halves)

    rows = tokens // 4

    def stepped(kernel, half, more):
        return pl.pallas_call(
            kernel,
            grid=(tokens // rows,),
            in_specs=[
                pl.BlockSpec((1, rows, width), lambda i: (half, i, 0)),
                pl.BlockSpec((1, late * lane, width), lambda i: (half, 0, 0)),
            ]
            + [pl.BlockSpec((rows, lane), lambda i: (i, 0))] * late
            + [pl.BlockSpec((rows, width), lambda i: (i, 0))] * more,
            out_specs=pl.BlockSpec((rows, width), lambda i: (i, 0)),
            out_shape=jax.ShapeDtypeStruct((tokens, width), BF),
            compiler_params=pltpu.CompilerParams(vmem_limit_bytes=12 * MIB),
            cost_estimate=pl.CostEstimate(
                flops=cost_us(1.5), bytes_accessed=8 * tokens * width, transcendentals=0
            ),
        )

    sent = swap(stepped(sent_kernel, 1, 0)(most, last, *row_gates[-late:]), "tp", 1)
    return stepped(final_kernel, 0, 2)(most, last, *row_gates[-late:], embedded, sent)


def solution(mesh):
    placed = (
        P("seq"),
        P(None, "tp"),
        P(),
        P("seq", None, "tp"),
        P(None, None, "tp"),
        P("tp", None),
        P("tp"),
        P("tp", "seq"),
    )
    return jax.shard_map(
        body, mesh=mesh, in_specs=placed, out_specs=P("seq", "tp"), check_vma=False
    )
```

```python
import functools

import jax
import jax.numpy as jnp
from jax import lax
from jax.experimental import pallas as pl
from jax.experimental.pallas import tpu as pltpu
from jax.sharding import PartitionSpec as P

BF = jnp.bfloat16
F32 = jnp.float32
MIB = 1024 * 1024
WHOLE = pl.BlockSpec(memory_space=pltpu.VMEM)
SCALARS = pl.BlockSpec(memory_space=pltpu.SMEM)


def swap(block, axis, offset):
    count = lax.axis_size(axis)
    return lax.ppermute(block, axis, [(i, i ^ offset) for i in range(count)])


def cost_us(time):
    return int(time * 1.1e9)


def call(kernel, out_shape, count, flops, moved, room=12, **more):
    return pl.pallas_call(
        kernel,
        out_shape=out_shape,
        in_specs=more.pop("in_specs", [WHOLE] * count),
        compiler_params=pltpu.CompilerParams(vmem_limit_bytes=room * MIB),
        cost_estimate=pl.CostEstimate(flops=flops, bytes_accessed=moved, transcendentals=0),
        **more,
    )


def after(value, *earlier):
    return lax.optimization_barrier((value, earlier))[0]


def turn_kernel(where_ref, weight_ref, *refs):
    out_refs, (held_ref, turned_ref, sems) = refs[:-3], refs[-3:]
    top = len(out_refs)
    rows = out_refs[0].shape[1]
    piece = rows // 3
    copies = [
        pltpu.make_async_copy(weight_ref.at[s], held_ref.at[s], sems.at[s]) for s in range(3)
    ]
    for copy in copies:
        copy.start()
    for s, copy in enumerate(copies):
        copy.wait()
        turned_ref[...] = held_ref[s].astype(F32).T.astype(BF).reshape(turned_ref.shape)
        for offset, out_ref in enumerate(out_refs):
            for far in range(2):
                place = where_ref[0] ^ (offset + far * top)
                out_ref[far, s * piece : (s + 1) * piece, :] = turned_ref[place]


def onehot(ids, vocab):
    entries = lax.broadcasted_iota(jnp.int32, (ids.shape[0], vocab), 1)
    return (entries == ids).astype(F32).astype(BF)


def embed_kernel(ids_ref, table_ref, out_ref):
    halo = ids_ref.shape[0] - out_ref.shape[0]
    out_ref[...] = jnp.dot(
        onehot(ids_ref[halo:, :], table_ref.shape[0]), table_ref[...], preferred_element_type=F32
    ).astype(BF)


def bands(line):
    taps = line.shape[1]
    row = lax.broadcasted_iota(jnp.int32, (taps, taps), 0)
    col = lax.broadcasted_iota(jnp.int32, (taps, taps), 1)
    ring = pltpu.roll(jnp.broadcast_to(line.astype(F32), (taps, taps)), 0, 1, stride=1, stride_axis=0)
    return jnp.concatenate(
        [jnp.where(col < row, ring, 0.0), jnp.where(col >= row, ring, 0.0)], axis=0
    ).astype(BF)


def norm_kernel(where_ref, gain_ref, *refs):
    blocks, out_ref, kept_ref, sem = refs[:-3], refs[-3], refs[-2], refs[-1]
    pieces, _, depth = out_ref.shape
    each = pieces // len(blocks)
    total = 0.0
    for block in blocks:
        wide = block[...].astype(F32)
        total = total + jnp.sum(wide * wide, axis=1, keepdims=True)
    scale = lax.rsqrt(total / (len(blocks) * blocks[0].shape[1]) + 1e-06)
    for j, block in enumerate(blocks):
        place = where_ref[1] ^ j
        result = (block[...].astype(F32) * scale * gain_ref[place]).astype(BF)
        for r in range(each):
            kept_ref[place * each + r] = result[:, r * depth : (r + 1) * depth]
    copy = pltpu.make_async_copy(kept_ref, out_ref, sem)
    copy.start()
    copy.wait()


def project_kernel(where_ref, normed_ref, crossing_ref, *refs):
    parts, out_ref, kept_ref, sem = refs[:-3], refs[-3], refs[-2], refs[-1]
    top = len(parts)
    copy = pltpu.make_async_copy(normed_ref, kept_ref, sem)
    copy.start()
    copy.wait()
    total = jnp.zeros(out_ref.shape, F32)
    for offset in range(2 * top):
        weight = parts[offset][0] if offset < top else crossing_ref[offset - top]
        total = total + lax.dot_general(
            weight,
            kept_ref[where_ref[0] ^ offset],
            (((1,), (1,)), ((), ())),
            preferred_element_type=F32,
        )
    out_ref[...] = total.astype(BF)


def mixer_kernel(
    group_size, where_ref, ids_ref, short_ref, skip_ref, filter_ref, *refs
):
    pieces = refs[:-6]
    out_ref, rows_ref, proj_ref, product_ref, turned_ref, conv_ref = refs[-6:]
    tokens, width = out_ref.shape
    short_taps = short_ref.shape[0]
    taps = filter_ref.shape[1]
    length, vocab = ids_ref.shape[0], rows_ref.shape[1]
    halo = length - tokens
    piece = width // len(pieces)
    blocks = tokens // taps
    for p, block in enumerate(pieces):
        place = (where_ref[0] & (len(pieces) - 1)) ^ p
        for s in range(3):
            begin = pl.multiple_of(s * width + place * piece, piece)
            rows_ref[pl.ds(begin, piece), :] = block[s * piece : (s + 1) * piece, :]
    step = 2 * taps
    for begin in range(0, length, step):
        count = min(step, length - begin)
        result = lax.dot_general(
            onehot(ids_ref[begin : begin + count, :], vocab),
            rows_ref[...],
            (((1,), (1,)), ((), ())),
            preferred_element_type=F32,
        )
        for s in range(3):
            proj_ref[s, begin : begin + count, :] = result[:, s * width : (s + 1) * width]

    def taken(s, begin):
        total = short_ref[0, s : s + 1, :] * proj_ref[s, begin : begin + taps, :]
        for lag in range(1, short_taps):
            total = total + short_ref[lag, s : s + 1, :] * proj_ref[s, begin - lag : begin - lag + taps, :]
        return total

    for b in range(blocks + 1):
        begin = halo + (b - 1) * taps
        product = (taken(1, begin) * taken(2, begin)).astype(BF).astype(F32)
        product_ref[b * taps : (b + 1) * taps, :] = product
        turned_ref[:, b * taps : (b + 1) * taps] = product.T.astype(BF)
    for g in range(width // group_size):
        rows = slice(g * group_size, (g + 1) * group_size)
        stacked = jnp.concatenate(
            [turned_ref[rows, b * taps : (b + 2) * taps] for b in range(blocks)], axis=0
        )
        mixed = jnp.dot(
            stacked, bands(filter_ref[g : g + 1, :]), preferred_element_type=F32
        )
        for b in range(blocks):
            conv_ref[rows, b * taps : (b + 1) * taps] = mixed[b * group_size : (b + 1) * group_size]
    for b in range(blocks):
        conv = conv_ref[:, b * taps : (b + 1) * taps].T
        conv = conv + skip_ref[...] * product_ref[(b + 1) * taps : (b + 2) * taps, :]
        gated = taken(0, halo + b * taps) * conv
        out_ref[b * taps : (b + 1) * taps, :] = gated.astype(BF)


def most_kernel(chunks, late, where_ref, *refs):
    count = 2 * chunks - late
    gates, weights, (out_ref, last_ref, lhs_ref, rhs_ref, sems) = refs[:count], refs[count:-5], refs[-5:]
    tokens, lane = gates[0].shape
    width = chunks * lane
    top, _, cols = rhs_ref.shape
    copies = []
    for index, weight in enumerate(weights):
        offset, side = index // 2, index % 2
        place = rhs_ref.at[offset ^ where_ref[4], pl.ds(side * width, width)]
        copies.append(pltpu.make_async_copy(weight, place, sems.at[index]))
        copies[-1].start()
    for index in range(2 * chunks):
        side, m = index // chunks, index % chunks
        begin = pl.multiple_of(side * width + (where_ref[2] ^ m) * lane, lane)
        if index < count:
            lhs_ref[:, pl.ds(begin, lane)] = gates[index][...]
        else:
            lhs_ref[:, pl.ds(begin, lane)] = jnp.zeros((tokens, lane), BF)
    for copy in copies:
        copy.wait()
    rows = min(tokens, 256)
    for half in range(2):
        for b in range(top // 2):
            place = (where_ref[3] ^ half) * (top // 2) + b
            at = slice(b * cols, (b + 1) * cols)
            for late_index in range(late):
                begin = width + (where_ref[2] ^ (chunks - late + late_index)) * lane
                last_ref[half, late_index * lane : (late_index + 1) * lane, at] = rhs_ref[
                    place, pl.ds(pl.multiple_of(begin, lane), lane), :
                ]
            for begin in range(0, tokens, rows):
                out_ref[half, begin : begin + rows, at] = jnp.dot(
                    lhs_ref[begin : begin + rows, :], rhs_ref[place], preferred_element_type=F32
                ).astype(out_ref.dtype)


def with_late(most_ref, weight_ref, gates):
    total = most_ref[0].astype(F32)
    lane = gates[0].shape[1]
    for index, gate in enumerate(gates):
        weight = weight_ref[0, index * lane : (index + 1) * lane, :]
        total = total + jnp.dot(gate[...], weight, preferred_element_type=F32)
    return total


def sent_kernel(most_ref, weight_ref, *refs):
    gates, out_ref = refs[:-1], refs[-1]
    out_ref[...] = with_late(most_ref, weight_ref, gates).astype(BF)


def final_kernel(most_ref, weight_ref, *refs):
    gates, (embed_ref, other_ref, out_ref) = refs[:-3], refs[-3:]
    own = with_late(most_ref, weight_ref, gates)
    out_ref[...] = (embed_ref[...].astype(F32) + own + other_ref[...].astype(F32)).astype(BF)


def body(
    token_ids, embed_table, norm_gain, in_weight, short_filter, long_filter, long_skip, out_weight
):
    chunks = 4
    n, minor = 2 * chunks, lax.axis_size("seq") // (2 * chunks)
    device, tp, m = lax.axis_index("seq"), lax.axis_index("tp"), lax.axis_size("tp")
    seq = device // minor
    tokens = token_ids.shape[0]
    vocab, width = embed_table.shape
    groups, taps = long_filter.shape
    short_taps = short_filter.shape[0]
    piece = width // n
    per_chunk = n // chunks
    lane = per_chunk * piece
    halo = taps + 16 * -(-(short_taps - 1) // 16)
    length = tokens + halo
    top = n // 2
    upper = (seq >= top).astype(jnp.int32)
    core, row = tp & 1, tp >> 1
    same_side = row == upper
    chunk_at = seq // per_chunk
    where = jnp.stack([seq, tp, chunk_at, core, seq & (top - 1)]).astype(jnp.int32)

    def over(block, offset):
        return swap(block, "seq", offset * minor)

    if minor > 1:
        parts = [[g * minor + j for j in range(minor)] for g in range(n)]
        in_weight = lax.all_gather(in_weight, "seq", axis=0, tiled=True, axis_index_groups=parts)
        out_weight = lax.all_gather(out_weight, "seq", axis=1, tiled=True, axis_index_groups=parts)
    depth = in_weight.shape[0]

    near = [out_weight]
    far = [over(out_weight, top)]

    parts = call(
        turn_kernel,
        [jax.ShapeDtypeStruct((2, 3 * piece, depth), BF)] * top,
        2,
        cost_us(1.0),
        4 * 3 * width * depth,
        in_specs=[SCALARS, pl.BlockSpec(memory_space=pltpu.HBM)],
        scratch_shapes=[
            pltpu.VMEM((3, depth, width), BF),
            pltpu.VMEM((n, piece, depth), BF),
            pltpu.SemaphoreType.DMA((3,)),
        ],
    )(where, in_weight.transpose(1, 0, 2))
    parts = [over(part, offset) if offset else part for offset, part in enumerate(parts)]

    table_row = swap(embed_table, "tp", 2)
    table_core = swap(after(embed_table, far[0]), "tp", 1)
    table_both = swap(table_row, "tp", 1)

    crossing = after(jnp.stack([part[1] for part in parts]), far[0], table_row, table_core)
    crossing = over(crossing, top)

    tail = lax.ppermute(after(token_ids, table_both)[tokens - halo :], "seq", [(i, i + 1) for i in range(n * minor - 1)])
    tail = jnp.where(device == 0, -1, tail)
    ids = jnp.concatenate([tail, token_ids])[:, None]

    near.append(over(near[0], 2))
    far.append(over(far[0], 2))
    normed = call(
        norm_kernel,
        jax.ShapeDtypeStruct((n, vocab, depth), BF),
        6,
        cost_us(1.5),
        4 * m * vocab * width,
        in_specs=[SCALARS] + [WHOLE] * 5,
        out_specs=pl.BlockSpec(memory_space=pltpu.HBM),
        scratch_shapes=[pltpu.VMEM((n, vocab, depth), BF), pltpu.SemaphoreType.DMA],
    )(where, norm_gain.reshape(m, 1, width), embed_table, table_core, table_row, table_both)

    parts[0] = after(parts[0], ids)
    projected = call(
        project_kernel,
        jax.ShapeDtypeStruct((3 * piece, vocab), BF),
        3,
        cost_us(10.0),
        2 * m * width * (vocab + 3 * piece),
        in_specs=[SCALARS, pl.BlockSpec(memory_space=pltpu.HBM)] + [WHOLE] * (top + 1),
        scratch_shapes=[pltpu.VMEM((n, vocab, depth), BF), pltpu.SemaphoreType.DMA],
    )(where, normed, crossing, *parts)

    embedded = call(
        embed_kernel, jax.ShapeDtypeStruct((tokens, width), BF), 2, cost_us(1.0), 2 * tokens * width
    )(ids, embed_table)
    halves = []
    for index, (one, two) in enumerate(zip(near, far, strict=True)):
        if index:
            one, two = after(one, projected), after(two, projected)
        kept = jnp.where(same_side, one, two)
        given = jnp.where(same_side, two, one)
        given = swap(given, "tp", 2)
        halves += [kept, given, over(kept, 1), over(given, 1)]

    halves[-1] = over(after(halves[-3], projected), 1)
    starts = [projected, over(projected, 2), over(projected, top)]
    gates, row_gates, besides = [], [], []
    for index in range(chunks):
        if index == 1:
            starts[2] = after(starts[2], gates[0])
            starts.append(over(starts[2], 2))
        pieces = [starts[index], over(starts[index], 1) if index < 3 else over(besides[2], 2)]
        besides.append(pieces[1])
        at = jnp.stack([seq, chunk_at ^ index]).astype(jnp.int32)
        if index == 2:
            at = after(at, row_gates[0])
        if index == 0:
            at = after(at, *halves[:6])
        gate = pl.pallas_call(
            functools.partial(mixer_kernel, width // groups),
            grid_spec=pltpu.PrefetchScalarGridSpec(
                num_scalar_prefetch=1,
                grid=(1,),
                in_specs=[
                    pl.BlockSpec((length, 1), lambda i, s: (0, 0)),
                    pl.BlockSpec((short_taps, 3, lane), lambda i, s: (0, 0, s[1])),
                    pl.BlockSpec((1, lane), lambda i, s: (0, s[1])),
                    pl.BlockSpec((lane * groups // width, taps), lambda i, s: (s[1], 0)),
                ]
                + [pl.BlockSpec((3 * piece, vocab), lambda i, s: (0, 0))] * len(pieces),
                out_specs=pl.BlockSpec((tokens, lane), lambda i, s: (0, 0)),
                scratch_shapes=[
                    pltpu.VMEM((3 * lane, vocab), BF),
                    pltpu.VMEM((3, length, lane), F32),
                    pltpu.VMEM((tokens + taps, lane), F32),
                    pltpu.VMEM((lane, tokens + taps), BF),
                    pltpu.VMEM((lane, tokens), F32),
                ],
            ),
            out_shape=jax.ShapeDtypeStruct((tokens, lane), BF),
            compiler_params=pltpu.CompilerParams(vmem_limit_bytes=12 * MIB),
            cost_estimate=pl.CostEstimate(
                flops=cost_us(3.5), bytes_accessed=4 * vocab * length, transcendentals=0
            ),
        )(at, ids, short_filter, long_skip[None, :], long_filter, *pieces)
        gates.append(gate)
        row_gates.append(swap(gate, "tp", 2))

    late = 2
    most, last = call(
        functools.partial(most_kernel, chunks, late),
        [
            jax.ShapeDtypeStruct((2, tokens, width), BF),
            jax.ShapeDtypeStruct((2, late * lane, width), BF),
        ],
        0,
        cost_us(4.0),
        8 * tokens * width,
        room=24,
        in_specs=[SCALARS]
        + [WHOLE] * (2 * chunks - late)
        + [pl.BlockSpec(memory_space=pltpu.HBM)] * (2 * top),
        scratch_shapes=[
            pltpu.VMEM((tokens, 2 * width), BF),
            pltpu.VMEM((top, 2 * width, width * 2 // top), BF),
            pltpu.SemaphoreType.DMA((2 * top,)),
        ],
    )(where, *gates, *row_gates[:-late], *halves)

    rows = tokens // 4

    def stepped(kernel, half, more):
        return pl.pallas_call(
            kernel,
            grid=(tokens // rows,),
            in_specs=[
                pl.BlockSpec((1, rows, width), lambda i: (half, i, 0)),
                pl.BlockSpec((1, late * lane, width), lambda i: (half, 0, 0)),
            ]
            + [pl.BlockSpec((rows, lane), lambda i: (i, 0))] * late
            + [pl.BlockSpec((rows, width), lambda i: (i, 0))] * more,
            out_specs=pl.BlockSpec((rows, width), lambda i: (i, 0)),
            out_shape=jax.ShapeDtypeStruct((tokens, width), BF),
            compiler_params=pltpu.CompilerParams(vmem_limit_bytes=12 * MIB),
            cost_estimate=pl.CostEstimate(
                flops=cost_us(1.5), bytes_accessed=8 * tokens * width, transcendentals=0
            ),
        )

    sent = swap(stepped(sent_kernel, 1, 0)(most, last, *row_gates[-late:]), "tp", 1)
    return stepped(final_kernel, 0, 2)(most, last, *row_gates[-late:], embedded, sent)


def solution(mesh):
    placed = (
        P("seq"),
        P(None, "tp"),
        P(),
        P("seq", None, "tp"),
        P(None, None, "tp"),
        P("tp", None),
        P("tp"),
        P("tp", "seq"),
    )
    return jax.shard_map(
        body, mesh=mesh, in_specs=placed, out_specs=P("seq", "tp"), check_vma=False
    )
```

```python
import functools

import jax
import jax.numpy as jnp
from jax import lax
from jax.experimental import pallas as pl
from jax.experimental.pallas import tpu as pltpu
from jax.sharding import PartitionSpec as P

BF = jnp.bfloat16
F32 = jnp.float32
MIB = 1024 * 1024
WHOLE = pl.BlockSpec(memory_space=pltpu.VMEM)
SCALARS = pl.BlockSpec(memory_space=pltpu.SMEM)


def swap(block, axis, offset):
    count = lax.axis_size(axis)
    return lax.ppermute(block, axis, [(i, i ^ offset) for i in range(count)])


def cost_us(time):
    return int(time * 1.1e9)


def call(kernel, out_shape, count, flops, moved, room=12, **more):
    return pl.pallas_call(
        kernel,
        out_shape=out_shape,
        in_specs=more.pop("in_specs", [WHOLE] * count),
        compiler_params=pltpu.CompilerParams(vmem_limit_bytes=room * MIB),
        cost_estimate=pl.CostEstimate(flops=flops, bytes_accessed=moved, transcendentals=0),
        **more,
    )


def after(value, *earlier):
    return lax.optimization_barrier((value, earlier))[0]


def turn_kernel(where_ref, weight_ref, *refs):
    out_refs, (held_ref, turned_ref, sems) = refs[:-3], refs[-3:]
    top = len(out_refs)
    rows = out_refs[0].shape[1]
    piece = rows // 3
    copies = [
        pltpu.make_async_copy(weight_ref.at[s], held_ref.at[s], sems.at[s]) for s in range(3)
    ]
    for copy in copies:
        copy.start()
    for s, copy in enumerate(copies):
        copy.wait()
        turned_ref[...] = held_ref[s].astype(F32).T.astype(BF).reshape(turned_ref.shape)
        for offset, out_ref in enumerate(out_refs):
            for far in range(2):
                place = where_ref[0] ^ (offset + far * top)
                out_ref[far, s * piece : (s + 1) * piece, :] = turned_ref[place]


def onehot(ids, vocab):
    entries = lax.broadcasted_iota(jnp.int32, (ids.shape[0], vocab), 1)
    return (entries == ids).astype(F32).astype(BF)


def embed_kernel(ids_ref, table_ref, out_ref):
    halo = ids_ref.shape[0] - out_ref.shape[0]
    out_ref[...] = jnp.dot(
        onehot(ids_ref[halo:, :], table_ref.shape[0]), table_ref[...], preferred_element_type=F32
    ).astype(BF)


def bands(line):
    taps = line.shape[1]
    row = lax.broadcasted_iota(jnp.int32, (taps, taps), 0)
    col = lax.broadcasted_iota(jnp.int32, (taps, taps), 1)
    ring = pltpu.roll(jnp.broadcast_to(line.astype(F32), (taps, taps)), 0, 1, stride=1, stride_axis=0)
    return jnp.concatenate(
        [jnp.where(col < row, ring, 0.0), jnp.where(col >= row, ring, 0.0)], axis=0
    ).astype(BF)


def norm_kernel(where_ref, gain_ref, *refs):
    blocks, out_ref, kept_ref, sem = refs[:-3], refs[-3], refs[-2], refs[-1]
    pieces, _, depth = out_ref.shape
    each = pieces // len(blocks)
    total = 0.0
    for block in blocks:
        wide = block[...].astype(F32)
        total = total + jnp.sum(wide * wide, axis=1, keepdims=True)
    scale = lax.rsqrt(total / (len(blocks) * blocks[0].shape[1]) + 1e-06)
    for j, block in enumerate(blocks):
        place = where_ref[1] ^ j
        result = (block[...].astype(F32) * scale * gain_ref[place]).astype(BF)
        for r in range(each):
            kept_ref[place * each + r] = result[:, r * depth : (r + 1) * depth]
    copy = pltpu.make_async_copy(kept_ref, out_ref, sem)
    copy.start()
    copy.wait()


def project_kernel(where_ref, normed_ref, crossing_ref, *refs):
    parts, out_ref, kept_ref, sem = refs[:-3], refs[-3], refs[-2], refs[-1]
    top = len(parts)
    copy = pltpu.make_async_copy(normed_ref, kept_ref, sem)
    copy.start()
    copy.wait()
    total = jnp.zeros(out_ref.shape, F32)
    for offset in range(2 * top):
        weight = parts[offset][0] if offset < top else crossing_ref[offset - top]
        total = total + lax.dot_general(
            weight,
            kept_ref[where_ref[0] ^ offset],
            (((1,), (1,)), ((), ())),
            preferred_element_type=F32,
        )
    out_ref[...] = total.astype(BF)


def mixer_kernel(
    group_size, where_ref, ids_ref, short_ref, skip_ref, filter_ref, *refs
):
    pieces = refs[:-6]
    out_ref, rows_ref, proj_ref, product_ref, turned_ref, conv_ref = refs[-6:]
    tokens, width = out_ref.shape
    short_taps = short_ref.shape[0]
    taps = filter_ref.shape[1]
    length, vocab = ids_ref.shape[0], rows_ref.shape[1]
    halo = length - tokens
    piece = width // len(pieces)
    blocks = tokens // taps
    for p, block in enumerate(pieces):
        place = (where_ref[0] & (len(pieces) - 1)) ^ p
        for s in range(3):
            begin = pl.multiple_of(s * width + place * piece, piece)
            rows_ref[pl.ds(begin, piece), :] = block[s * piece : (s + 1) * piece, :]
    step = 2 * taps
    for begin in range(0, length, step):
        count = min(step, length - begin)
        result = lax.dot_general(
            onehot(ids_ref[begin : begin + count, :], vocab),
            rows_ref[...],
            (((1,), (1,)), ((), ())),
            preferred_element_type=F32,
        )
        for s in range(3):
            proj_ref[s, begin : begin + count, :] = result[:, s * width : (s + 1) * width]

    def taken(s, begin):
        total = short_ref[0, s : s + 1, :] * proj_ref[s, begin : begin + taps, :]
        for lag in range(1, short_taps):
            total = total + short_ref[lag, s : s + 1, :] * proj_ref[s, begin - lag : begin - lag + taps, :]
        return total

    for b in range(blocks + 1):
        begin = halo + (b - 1) * taps
        product = (taken(1, begin) * taken(2, begin)).astype(BF).astype(F32)
        product_ref[b * taps : (b + 1) * taps, :] = product
        turned_ref[:, b * taps : (b + 1) * taps] = product.T.astype(BF)
    for g in range(width // group_size):
        rows = slice(g * group_size, (g + 1) * group_size)
        stacked = jnp.concatenate(
            [turned_ref[rows, b * taps : (b + 2) * taps] for b in range(blocks)], axis=0
        )
        mixed = jnp.dot(
            stacked, bands(filter_ref[g : g + 1, :]), preferred_element_type=F32
        )
        for b in range(blocks):
            conv_ref[rows, b * taps : (b + 1) * taps] = mixed[b * group_size : (b + 1) * group_size]
    for b in range(blocks):
        conv = conv_ref[:, b * taps : (b + 1) * taps].T
        conv = conv + skip_ref[...] * product_ref[(b + 1) * taps : (b + 2) * taps, :]
        gated = taken(0, halo + b * taps) * conv
        out_ref[b * taps : (b + 1) * taps, :] = gated.astype(BF)


def most_kernel(chunks, late, where_ref, *refs):
    count = 2 * chunks - late
    gates, weights, (out_ref, last_ref, lhs_ref, rhs_ref, sems) = refs[:count], refs[count:-5], refs[-5:]
    tokens, lane = gates[0].shape
    width = chunks * lane
    top, _, cols = rhs_ref.shape
    copies = []
    for index, weight in enumerate(weights):
        offset, side = index // 2, index % 2
        place = rhs_ref.at[offset ^ where_ref[4], pl.ds(side * width, width)]
        copies.append(pltpu.make_async_copy(weight, place, sems.at[index]))
        copies[-1].start()
    for index in range(2 * chunks):
        side, m = index // chunks, index % chunks
        begin = pl.multiple_of(side * width + (where_ref[2] ^ m) * lane, lane)
        if index < count:
            lhs_ref[:, pl.ds(begin, lane)] = gates[index][...]
        else:
            lhs_ref[:, pl.ds(begin, lane)] = jnp.zeros((tokens, lane), BF)
    for copy in copies:
        copy.wait()
    rows = min(tokens, 256)
    for half in range(2):
        for b in range(top // 2):
            place = (where_ref[3] ^ half) * (top // 2) + b
            at = slice(b * cols, (b + 1) * cols)
            for late_index in range(late):
                begin = width + (where_ref[2] ^ (chunks - late + late_index)) * lane
                last_ref[half, late_index * lane : (late_index + 1) * lane, at] = rhs_ref[
                    place, pl.ds(pl.multiple_of(begin, lane), lane), :
                ]
            for begin in range(0, tokens, rows):
                out_ref[half, begin : begin + rows, at] = jnp.dot(
                    lhs_ref[begin : begin + rows, :], rhs_ref[place], preferred_element_type=F32
                ).astype(out_ref.dtype)


def with_late(most_ref, weight_ref, gates):
    total = most_ref[0].astype(F32)
    lane = gates[0].shape[1]
    for index, gate in enumerate(gates):
        weight = weight_ref[0, index * lane : (index + 1) * lane, :]
        total = total + jnp.dot(gate[...], weight, preferred_element_type=F32)
    return total


def sent_kernel(most_ref, weight_ref, *refs):
    gates, out_ref = refs[:-1], refs[-1]
    out_ref[...] = with_late(most_ref, weight_ref, gates).astype(BF)


def final_kernel(most_ref, weight_ref, *refs):
    gates, (embed_ref, other_ref, out_ref) = refs[:-3], refs[-3:]
    own = with_late(most_ref, weight_ref, gates)
    out_ref[...] = (embed_ref[...].astype(F32) + own + other_ref[...].astype(F32)).astype(BF)


def body(
    token_ids, embed_table, norm_gain, in_weight, short_filter, long_filter, long_skip, out_weight
):
    chunks = 4
    n, minor = 2 * chunks, lax.axis_size("seq") // (2 * chunks)
    device, tp, m = lax.axis_index("seq"), lax.axis_index("tp"), lax.axis_size("tp")
    seq = device // minor
    tokens = token_ids.shape[0]
    vocab, width = embed_table.shape
    groups, taps = long_filter.shape
    short_taps = short_filter.shape[0]
    piece = width // n
    per_chunk = n // chunks
    lane = per_chunk * piece
    halo = taps + 16 * -(-(short_taps - 1) // 16)
    length = tokens + halo
    top = n // 2
    upper = (seq >= top).astype(jnp.int32)
    core, row = tp & 1, tp >> 1
    same_side = row == upper
    chunk_at = seq // per_chunk
    where = jnp.stack([seq, tp, chunk_at, core, seq & (top - 1)]).astype(jnp.int32)

    def over(block, offset):
        return swap(block, "seq", offset * minor)

    if minor > 1:
        parts = [[g * minor + j for j in range(minor)] for g in range(n)]
        in_weight = lax.all_gather(in_weight, "seq", axis=0, tiled=True, axis_index_groups=parts)
        out_weight = lax.all_gather(out_weight, "seq", axis=1, tiled=True, axis_index_groups=parts)
    depth = in_weight.shape[0]

    near = [out_weight]
    far = [over(out_weight, top)]

    parts = call(
        turn_kernel,
        [jax.ShapeDtypeStruct((2, 3 * piece, depth), BF)] * top,
        2,
        cost_us(1.0),
        4 * 3 * width * depth,
        in_specs=[SCALARS, pl.BlockSpec(memory_space=pltpu.HBM)],
        scratch_shapes=[
            pltpu.VMEM((3, depth, width), BF),
            pltpu.VMEM((n, piece, depth), BF),
            pltpu.SemaphoreType.DMA((3,)),
        ],
    )(where, in_weight.transpose(1, 0, 2))
    parts = [over(part, offset) if offset else part for offset, part in enumerate(parts)]

    table_row = swap(embed_table, "tp", 2)
    table_core = swap(after(embed_table, far[0]), "tp", 1)
    table_both = swap(table_row, "tp", 1)

    crossing = after(jnp.stack([part[1] for part in parts]), far[0], table_row, table_core)
    crossing = over(crossing, top)

    tail = lax.ppermute(after(token_ids, table_both)[tokens - halo :], "seq", [(i, i + 1) for i in range(n * minor - 1)])
    tail = jnp.where(device == 0, -1, tail)
    ids = jnp.concatenate([tail, token_ids])[:, None]

    near.append(over(near[0], 2))
    far.append(over(far[0], 2))
    normed = call(
        norm_kernel,
        jax.ShapeDtypeStruct((n, vocab, depth), BF),
        6,
        cost_us(1.5),
        4 * m * vocab * width,
        in_specs=[SCALARS] + [WHOLE] * 5,
        out_specs=pl.BlockSpec(memory_space=pltpu.HBM),
        scratch_shapes=[pltpu.VMEM((n, vocab, depth), BF), pltpu.SemaphoreType.DMA],
    )(where, norm_gain.reshape(m, 1, width), embed_table, table_core, table_row, table_both)

    parts[0] = after(parts[0], ids)
    projected = call(
        project_kernel,
        jax.ShapeDtypeStruct((3 * piece, vocab), BF),
        3,
        cost_us(10.0),
        2 * m * width * (vocab + 3 * piece),
        in_specs=[SCALARS, pl.BlockSpec(memory_space=pltpu.HBM)] + [WHOLE] * (top + 1),
        scratch_shapes=[pltpu.VMEM((n, vocab, depth), BF), pltpu.SemaphoreType.DMA],
    )(where, normed, crossing, *parts)

    embedded = call(
        embed_kernel, jax.ShapeDtypeStruct((tokens, width), BF), 2, cost_us(1.0), 2 * tokens * width
    )(ids, embed_table)
    halves = []
    for index, (one, two) in enumerate(zip(near, far, strict=True)):
        if index:
            one, two = after(one, projected), after(two, projected)
        kept = jnp.where(same_side, one, two)
        given = jnp.where(same_side, two, one)
        given = swap(given, "tp", 2)
        halves += [kept, given, over(kept, 1), over(given, 1)]

    halves[-1] = over(after(halves[-3], projected), 1)
    starts = [projected, over(projected, 2), over(projected, top)]
    gates, row_gates, besides = [], [], []
    for index in range(chunks):
        if index == 1:
            starts[2] = after(starts[2], gates[0])
            starts[1] = after(starts[1], gates[0])
            starts.append(over(starts[2], 2))
        pieces = [starts[index], over(starts[index], 1) if index < 3 else over(besides[2], 2)]
        besides.append(pieces[1])
        at = jnp.stack([seq, chunk_at ^ index]).astype(jnp.int32)
        if index == 2:
            at = after(at, row_gates[0])
        if index == 1:
            at = after(at, *halves[:7])
        if index == 0:
            at = after(at, *halves[:6])
        gate = pl.pallas_call(
            functools.partial(mixer_kernel, width // groups),
            grid_spec=pltpu.PrefetchScalarGridSpec(
                num_scalar_prefetch=1,
                grid=(1,),
                in_specs=[
                    pl.BlockSpec((length, 1), lambda i, s: (0, 0)),
                    pl.BlockSpec((short_taps, 3, lane), lambda i, s: (0, 0, s[1])),
                    pl.BlockSpec((1, lane), lambda i, s: (0, s[1])),
                    pl.BlockSpec((lane * groups // width, taps), lambda i, s: (s[1], 0)),
                ]
                + [pl.BlockSpec((3 * piece, vocab), lambda i, s: (0, 0))] * len(pieces),
                out_specs=pl.BlockSpec((tokens, lane), lambda i, s: (0, 0)),
                scratch_shapes=[
                    pltpu.VMEM((3 * lane, vocab), BF),
                    pltpu.VMEM((3, length, lane), F32),
                    pltpu.VMEM((tokens + taps, lane), F32),
                    pltpu.VMEM((lane, tokens + taps), BF),
                    pltpu.VMEM((lane, tokens), F32),
                ],
            ),
            out_shape=jax.ShapeDtypeStruct((tokens, lane), BF),
            compiler_params=pltpu.CompilerParams(vmem_limit_bytes=12 * MIB),
            cost_estimate=pl.CostEstimate(
                flops=cost_us(3.5), bytes_accessed=4 * vocab * length, transcendentals=0
            ),
        )(at, ids, short_filter, long_skip[None, :], long_filter, *pieces)
        gates.append(gate)
        row_gates.append(swap(gate, "tp", 2))

    late = 2
    most, last = call(
        functools.partial(most_kernel, chunks, late),
        [
            jax.ShapeDtypeStruct((2, tokens, width), BF),
            jax.ShapeDtypeStruct((2, late * lane, width), BF),
        ],
        0,
        cost_us(4.0),
        8 * tokens * width,
        room=24,
        in_specs=[SCALARS]
        + [WHOLE] * (2 * chunks - late)
        + [pl.BlockSpec(memory_space=pltpu.HBM)] * (2 * top),
        scratch_shapes=[
            pltpu.VMEM((tokens, 2 * width), BF),
            pltpu.VMEM((top, 2 * width, width * 2 // top), BF),
            pltpu.SemaphoreType.DMA((2 * top,)),
        ],
    )(where, *gates, *row_gates[:-late], *halves)

    rows = tokens // 2

    def stepped(kernel, half, more):
        return pl.pallas_call(
            kernel,
            grid=(tokens // rows,),
            in_specs=[
                pl.BlockSpec((1, rows, width), lambda i: (half, i, 0)),
                pl.BlockSpec((1, late * lane, width), lambda i: (half, 0, 0)),
            ]
            + [pl.BlockSpec((rows, lane), lambda i: (i, 0))] * late
            + [pl.BlockSpec((rows, width), lambda i: (i, 0))] * more,
            out_specs=pl.BlockSpec((rows, width), lambda i: (i, 0)),
            out_shape=jax.ShapeDtypeStruct((tokens, width), BF),
            compiler_params=pltpu.CompilerParams(vmem_limit_bytes=12 * MIB),
            cost_estimate=pl.CostEstimate(
                flops=cost_us(1.5), bytes_accessed=8 * tokens * width, transcendentals=0
            ),
        )

    sent = swap(stepped(sent_kernel, 1, 0)(most, last, *row_gates[-late:]), "tp", 1)
    return stepped(final_kernel, 0, 2)(most, last, *row_gates[-late:], embedded, sent)


def solution(mesh):
    placed = (
        P("seq"),
        P(None, "tp"),
        P(),
        P("seq", None, "tp"),
        P(None, None, "tp"),
        P("tp", None),
        P("tp"),
        P("tp", "seq"),
    )
    return jax.shard_map(
        body, mesh=mesh, in_specs=placed, out_specs=P("seq", "tp"), check_vma=False
    )
```

```python
import functools

import jax
import jax.numpy as jnp
from jax import lax
from jax.experimental import pallas as pl
from jax.experimental.pallas import tpu as pltpu
from jax.sharding import PartitionSpec as P

BF = jnp.bfloat16
F32 = jnp.float32
MIB = 1024 * 1024
WHOLE = pl.BlockSpec(memory_space=pltpu.VMEM)
SCALARS = pl.BlockSpec(memory_space=pltpu.SMEM)


def swap(block, axis, offset):
    count = lax.axis_size(axis)
    return lax.ppermute(block, axis, [(i, i ^ offset) for i in range(count)])


def cost_us(time):
    return int(time * 1.1e9)


def call(kernel, out_shape, count, flops, moved, room=12, **more):
    return pl.pallas_call(
        kernel,
        out_shape=out_shape,
        in_specs=more.pop("in_specs", [WHOLE] * count),
        compiler_params=pltpu.CompilerParams(vmem_limit_bytes=room * MIB),
        cost_estimate=pl.CostEstimate(flops=flops, bytes_accessed=moved, transcendentals=0),
        **more,
    )


def after(value, *earlier):
    return lax.optimization_barrier((value, earlier))[0]


def turn_kernel(where_ref, weight_ref, *refs):
    out_refs, (held_ref, turned_ref, sems) = refs[:-3], refs[-3:]
    top = len(out_refs)
    rows = out_refs[0].shape[1]
    piece = rows // 3
    copies = [
        pltpu.make_async_copy(weight_ref.at[s], held_ref.at[s], sems.at[s]) for s in range(3)
    ]
    for copy in copies:
        copy.start()
    for s, copy in enumerate(copies):
        copy.wait()
        turned_ref[...] = held_ref[s].astype(F32).T.astype(BF).reshape(turned_ref.shape)
        for offset, out_ref in enumerate(out_refs):
            for far in range(2):
                place = where_ref[0] ^ (offset + far * top)
                out_ref[far, s * piece : (s + 1) * piece, :] = turned_ref[place]


def onehot(ids, vocab):
    entries = lax.broadcasted_iota(jnp.int32, (ids.shape[0], vocab), 1)
    return (entries == ids).astype(F32).astype(BF)


def embed_kernel(ids_ref, table_ref, out_ref):
    halo = ids_ref.shape[0] - out_ref.shape[0]
    out_ref[...] = jnp.dot(
        onehot(ids_ref[halo:, :], table_ref.shape[0]), table_ref[...], preferred_element_type=F32
    ).astype(BF)


def bands(line):
    taps = line.shape[1]
    row = lax.broadcasted_iota(jnp.int32, (taps, taps), 0)
    col = lax.broadcasted_iota(jnp.int32, (taps, taps), 1)
    ring = pltpu.roll(jnp.broadcast_to(line.astype(F32), (taps, taps)), 0, 1, stride=1, stride_axis=0)
    return jnp.concatenate(
        [jnp.where(col < row, ring, 0.0), jnp.where(col >= row, ring, 0.0)], axis=0
    ).astype(BF)


def norm_kernel(where_ref, gain_ref, *refs):
    blocks, out_ref, kept_ref, sem = refs[:-3], refs[-3], refs[-2], refs[-1]
    pieces, _, depth = out_ref.shape
    each = pieces // len(blocks)
    total = 0.0
    for block in blocks:
        wide = block[...].astype(F32)
        total = total + jnp.sum(wide * wide, axis=1, keepdims=True)
    scale = lax.rsqrt(total / (len(blocks) * blocks[0].shape[1]) + 1e-06)
    for j, block in enumerate(blocks):
        place = where_ref[1] ^ j
        result = (block[...].astype(F32) * scale * gain_ref[place]).astype(BF)
        for r in range(each):
            kept_ref[place * each + r] = result[:, r * depth : (r + 1) * depth]
    copy = pltpu.make_async_copy(kept_ref, out_ref, sem)
    copy.start()
    copy.wait()


def project_kernel(where_ref, normed_ref, crossing_ref, *refs):
    parts, out_ref, kept_ref, sem = refs[:-3], refs[-3], refs[-2], refs[-1]
    top = len(parts)
    copy = pltpu.make_async_copy(normed_ref, kept_ref, sem)
    copy.start()
    copy.wait()
    total = jnp.zeros(out_ref.shape, F32)
    for offset in range(2 * top):
        weight = parts[offset][0] if offset < top else crossing_ref[offset - top]
        total = total + lax.dot_general(
            weight,
            kept_ref[where_ref[0] ^ offset],
            (((1,), (1,)), ((), ())),
            preferred_element_type=F32,
        )
    out_ref[...] = total.astype(BF)


def mixer_kernel(
    group_size, where_ref, ids_ref, short_ref, skip_ref, filter_ref, *refs
):
    pieces = refs[:-6]
    out_ref, rows_ref, proj_ref, product_ref, turned_ref, conv_ref = refs[-6:]
    tokens, width = out_ref.shape
    short_taps = short_ref.shape[0]
    taps = filter_ref.shape[1]
    length, vocab = ids_ref.shape[0], rows_ref.shape[1]
    halo = length - tokens
    piece = width // len(pieces)
    blocks = tokens // taps
    for p, block in enumerate(pieces):
        place = (where_ref[0] & (len(pieces) - 1)) ^ p
        for s in range(3):
            begin = pl.multiple_of(s * width + place * piece, piece)
            rows_ref[pl.ds(begin, piece), :] = block[s * piece : (s + 1) * piece, :]
    step = 2 * taps
    for begin in range(0, length, step):
        count = min(step, length - begin)
        result = lax.dot_general(
            onehot(ids_ref[begin : begin + count, :], vocab),
            rows_ref[...],
            (((1,), (1,)), ((), ())),
            preferred_element_type=F32,
        )
        for s in range(3):
            proj_ref[s, begin : begin + count, :] = result[:, s * width : (s + 1) * width]

    def taken(s, begin):
        total = short_ref[0, s : s + 1, :] * proj_ref[s, begin : begin + taps, :]
        for lag in range(1, short_taps):
            total = total + short_ref[lag, s : s + 1, :] * proj_ref[s, begin - lag : begin - lag + taps, :]
        return total

    for b in range(blocks + 1):
        begin = halo + (b - 1) * taps
        product = (taken(1, begin) * taken(2, begin)).astype(BF).astype(F32)
        product_ref[b * taps : (b + 1) * taps, :] = product
        turned_ref[:, b * taps : (b + 1) * taps] = product.T.astype(BF)
    for g in range(width // group_size):
        rows = slice(g * group_size, (g + 1) * group_size)
        stacked = jnp.concatenate(
            [turned_ref[rows, b * taps : (b + 2) * taps] for b in range(blocks)], axis=0
        )
        mixed = jnp.dot(
            stacked, bands(filter_ref[g : g + 1, :]), preferred_element_type=F32
        )
        for b in range(blocks):
            conv_ref[rows, b * taps : (b + 1) * taps] = mixed[b * group_size : (b + 1) * group_size]
    for b in range(blocks):
        conv = conv_ref[:, b * taps : (b + 1) * taps].T
        conv = conv + skip_ref[...] * product_ref[(b + 1) * taps : (b + 2) * taps, :]
        gated = taken(0, halo + b * taps) * conv
        out_ref[b * taps : (b + 1) * taps, :] = gated.astype(BF)


def most_kernel(chunks, late, where_ref, *refs):
    count = 2 * chunks - late
    gates, weights, (out_ref, last_ref, lhs_ref, rhs_ref, sems) = refs[:count], refs[count:-5], refs[-5:]
    tokens, lane = gates[0].shape
    width = chunks * lane
    top, _, cols = rhs_ref.shape
    copies = []
    for index, weight in enumerate(weights):
        offset, side = index // 2, index % 2
        place = rhs_ref.at[offset ^ where_ref[4], pl.ds(side * width, width)]
        copies.append(pltpu.make_async_copy(weight, place, sems.at[index]))
        copies[-1].start()
    for index in range(2 * chunks):
        side, m = index // chunks, index % chunks
        begin = pl.multiple_of(side * width + (where_ref[2] ^ m) * lane, lane)
        if index < count:
            lhs_ref[:, pl.ds(begin, lane)] = gates[index][...]
        else:
            lhs_ref[:, pl.ds(begin, lane)] = jnp.zeros((tokens, lane), BF)
    for copy in copies:
        copy.wait()
    rows = min(tokens, 256)
    for half in range(2):
        for b in range(top // 2):
            place = (where_ref[3] ^ half) * (top // 2) + b
            at = slice(b * cols, (b + 1) * cols)
            for late_index in range(late):
                begin = width + (where_ref[2] ^ (chunks - late + late_index)) * lane
                last_ref[half, late_index * lane : (late_index + 1) * lane, at] = rhs_ref[
                    place, pl.ds(pl.multiple_of(begin, lane), lane), :
                ]
            for begin in range(0, tokens, rows):
                out_ref[half, begin : begin + rows, at] = jnp.dot(
                    lhs_ref[begin : begin + rows, :], rhs_ref[place], preferred_element_type=F32
                ).astype(out_ref.dtype)


def with_late(most_ref, weight_ref, gates):
    total = most_ref[0].astype(F32)
    lane = gates[0].shape[1]
    for index, gate in enumerate(gates):
        weight = weight_ref[0, index * lane : (index + 1) * lane, :]
        total = total + jnp.dot(gate[...], weight, preferred_element_type=F32)
    return total


def sent_kernel(most_ref, weight_ref, *refs):
    gates, out_ref = refs[:-1], refs[-1]
    out_ref[...] = with_late(most_ref, weight_ref, gates).astype(BF)


def final_kernel(most_ref, weight_ref, *refs):
    gates, (embed_ref, other_ref, out_ref) = refs[:-3], refs[-3:]
    own = with_late(most_ref, weight_ref, gates)
    out_ref[...] = (embed_ref[...].astype(F32) + own + other_ref[...].astype(F32)).astype(BF)


def body(
    token_ids, embed_table, norm_gain, in_weight, short_filter, long_filter, long_skip, out_weight
):
    chunks = 4
    n, minor = 2 * chunks, lax.axis_size("seq") // (2 * chunks)
    device, tp, m = lax.axis_index("seq"), lax.axis_index("tp"), lax.axis_size("tp")
    seq = device // minor
    tokens = token_ids.shape[0]
    vocab, width = embed_table.shape
    groups, taps = long_filter.shape
    short_taps = short_filter.shape[0]
    piece = width // n
    per_chunk = n // chunks
    lane = per_chunk * piece
    halo = taps + 16 * -(-(short_taps - 1) // 16)
    length = tokens + halo
    top = n // 2
    upper = (seq >= top).astype(jnp.int32)
    core, row = tp & 1, tp >> 1
    same_side = row == upper
    chunk_at = seq // per_chunk
    where = jnp.stack([seq, tp, chunk_at, core, seq & (top - 1)]).astype(jnp.int32)

    def over(block, offset):
        return swap(block, "seq", offset * minor)

    if minor > 1:
        parts = [[g * minor + j for j in range(minor)] for g in range(n)]
        in_weight = lax.all_gather(in_weight, "seq", axis=0, tiled=True, axis_index_groups=parts)
        out_weight = lax.all_gather(out_weight, "seq", axis=1, tiled=True, axis_index_groups=parts)
    depth = in_weight.shape[0]

    near = [out_weight]
    far = [over(out_weight, top)]

    parts = call(
        turn_kernel,
        [jax.ShapeDtypeStruct((2, 3 * piece, depth), BF)] * top,
        2,
        cost_us(1.0),
        4 * 3 * width * depth,
        in_specs=[SCALARS, pl.BlockSpec(memory_space=pltpu.HBM)],
        scratch_shapes=[
            pltpu.VMEM((3, depth, width), BF),
            pltpu.VMEM((n, piece, depth), BF),
            pltpu.SemaphoreType.DMA((3,)),
        ],
    )(where, in_weight.transpose(1, 0, 2))
    parts = [over(part, offset) if offset else part for offset, part in enumerate(parts)]

    table_row = swap(embed_table, "tp", 2)
    table_core = swap(after(embed_table, far[0]), "tp", 1)
    table_both = swap(table_row, "tp", 1)

    crossing = after(jnp.stack([part[1] for part in parts]), far[0], table_row, table_core)
    crossing = over(crossing, top)

    tail = lax.ppermute(after(token_ids, table_both)[tokens - halo :], "seq", [(i, i + 1) for i in range(n * minor - 1)])
    tail = jnp.where(device == 0, -1, tail)
    ids = jnp.concatenate([tail, token_ids])[:, None]

    near.append(over(near[0], 2))
    far.append(over(far[0], 2))
    normed = call(
        norm_kernel,
        jax.ShapeDtypeStruct((n, vocab, depth), BF),
        6,
        cost_us(1.5),
        4 * m * vocab * width,
        in_specs=[SCALARS] + [WHOLE] * 5,
        out_specs=pl.BlockSpec(memory_space=pltpu.HBM),
        scratch_shapes=[pltpu.VMEM((n, vocab, depth), BF), pltpu.SemaphoreType.DMA],
    )(where, norm_gain.reshape(m, 1, width), embed_table, table_core, table_row, table_both)

    parts[0] = after(parts[0], ids)
    projected = call(
        project_kernel,
        jax.ShapeDtypeStruct((3 * piece, vocab), BF),
        3,
        cost_us(10.0),
        2 * m * width * (vocab + 3 * piece),
        in_specs=[SCALARS, pl.BlockSpec(memory_space=pltpu.HBM)] + [WHOLE] * (top + 1),
        scratch_shapes=[pltpu.VMEM((n, vocab, depth), BF), pltpu.SemaphoreType.DMA],
    )(where, normed, crossing, *parts)

    embedded = call(
        embed_kernel, jax.ShapeDtypeStruct((tokens, width), BF), 2, cost_us(1.0), 2 * tokens * width
    )(ids, embed_table)
    halves = []
    for index, (one, two) in enumerate(zip(near, far, strict=True)):
        if index:
            one, two = after(one, projected), after(two, projected)
        kept = jnp.where(same_side, one, two)
        given = jnp.where(same_side, two, one)
        given = swap(given, "tp", 2)
        halves += [kept, given, over(kept, 1), over(given, 1)]

    halves[-1] = over(after(halves[-3], projected), 1)
    starts = [projected, over(projected, 2), over(projected, top)]
    gates, row_gates, besides = [], [], []
    for index in range(chunks):
        if index == 1:
            starts[2] = after(starts[2], gates[0])
            starts[1] = after(starts[1], gates[0])
            starts.append(over(starts[2], 2))
        pieces = [starts[index], over(starts[index], 1) if index < 3 else over(besides[2], 2)]
        besides.append(pieces[1])
        at = jnp.stack([seq, chunk_at ^ index]).astype(jnp.int32)
        if index == 2:
            at = after(at, row_gates[0])
        if index == 1:
            at = after(at, *halves[:7])
        if index == 0:
            at = after(at, *halves[:6])
        gate = pl.pallas_call(
            functools.partial(mixer_kernel, width // groups),
            grid_spec=pltpu.PrefetchScalarGridSpec(
                num_scalar_prefetch=1,
                grid=(1,),
                in_specs=[
                    pl.BlockSpec((length, 1), lambda i, s: (0, 0)),
                    pl.BlockSpec((short_taps, 3, lane), lambda i, s: (0, 0, s[1])),
                    pl.BlockSpec((1, lane), lambda i, s: (0, s[1])),
                    pl.BlockSpec((lane * groups // width, taps), lambda i, s: (s[1], 0)),
                ]
                + [pl.BlockSpec((3 * piece, vocab), lambda i, s: (0, 0))] * len(pieces),
                out_specs=pl.BlockSpec((tokens, lane), lambda i, s: (0, 0)),
                scratch_shapes=[
                    pltpu.VMEM((3 * lane, vocab), BF),
                    pltpu.VMEM((3, length, lane), F32),
                    pltpu.VMEM((tokens + taps, lane), F32),
                    pltpu.VMEM((lane, tokens + taps), BF),
                    pltpu.VMEM((lane, tokens), F32),
                ],
            ),
            out_shape=jax.ShapeDtypeStruct((tokens, lane), BF),
            compiler_params=pltpu.CompilerParams(vmem_limit_bytes=12 * MIB),
            cost_estimate=pl.CostEstimate(
                flops=cost_us(3.5), bytes_accessed=4 * vocab * length, transcendentals=0
            ),
        )(at, ids, short_filter, long_skip[None, :], long_filter, *pieces)
        gates.append(gate)
        row_gates.append(swap(gate, "tp", 2))

    late = 2
    most, last = call(
        functools.partial(most_kernel, chunks, late),
        [
            jax.ShapeDtypeStruct((2, tokens, width), BF),
            jax.ShapeDtypeStruct((2, late * lane, width), BF),
        ],
        0,
        cost_us(4.0),
        8 * tokens * width,
        room=24,
        in_specs=[SCALARS]
        + [WHOLE] * (2 * chunks - late)
        + [pl.BlockSpec(memory_space=pltpu.HBM)] * (2 * top),
        scratch_shapes=[
            pltpu.VMEM((tokens, 2 * width), BF),
            pltpu.VMEM((top, 2 * width, width * 2 // top), BF),
            pltpu.SemaphoreType.DMA((2 * top,)),
        ],
    )(where, *gates, *row_gates[:-late], *halves)

    rows = tokens

    def stepped(kernel, half, more):
        return pl.pallas_call(
            kernel,
            grid=(tokens // rows,),
            in_specs=[
                pl.BlockSpec((1, rows, width), lambda i: (half, i, 0)),
                pl.BlockSpec((1, late * lane, width), lambda i: (half, 0, 0)),
            ]
            + [pl.BlockSpec((rows, lane), lambda i: (i, 0))] * late
            + [pl.BlockSpec((rows, width), lambda i: (i, 0))] * more,
            out_specs=pl.BlockSpec((rows, width), lambda i: (i, 0)),
            out_shape=jax.ShapeDtypeStruct((tokens, width), BF),
            compiler_params=pltpu.CompilerParams(vmem_limit_bytes=40 * MIB),
            cost_estimate=pl.CostEstimate(
                flops=cost_us(1.5), bytes_accessed=8 * tokens * width, transcendentals=0
            ),
        )

    sent = swap(stepped(sent_kernel, 1, 0)(most, last, *row_gates[-late:]), "tp", 1)
    return stepped(final_kernel, 0, 2)(most, last, *row_gates[-late:], embedded, sent)


def solution(mesh):
    placed = (
        P("seq"),
        P(None, "tp"),
        P(),
        P("seq", None, "tp"),
        P(None, None, "tp"),
        P("tp", None),
        P("tp"),
        P("tp", "seq"),
    )
    return jax.shard_map(
        body, mesh=mesh, in_specs=placed, out_specs=P("seq", "tp"), check_vma=False
    )
```
